512 devices in a mesh: lon: 32 (over z_lo, y, core), lat: 16 (over z_hi, x).
Axes of the slice: x: 4, y: 8, z: 8 (z_hi: 4, z_lo: 2; z = z_hi * 2 + z_lo), core: 2. Of those that a mesh axis runs over, the one named last changes fastest.
Arguments:
- tokens: bfloat16 [384, 128, 1024], P('lon', 'lat'), may hold values from -6 to 6
- query_local: bfloat16 [384, 128, 1024], P('lon', 'lat'), may hold values from -21 to 21, as said below
- key_local: bfloat16 [384, 128, 1024], P('lon', 'lat'), may hold values from -21 to 21, as said below
- value_local: bfloat16 [384, 128, 1024], P('lon', 'lat'), may hold values from -6 to 6
- position_bias: float32 [16, 13, 13], replicated, may hold values from -4 to 4
- output_weight: bfloat16 [1024, 1024], P('lat'), may hold values from -0.1875 to 0.1875
- norm_gain: float32 [1024], replicated, may hold values from 0.1 to 1.9
- global_weight: bfloat16 [1024, 3072], P('lat'), may hold values from -1 to 1
Outputs:
- hidden: bfloat16 [384, 128, 1024], P('lon', 'lat')
- attended: bfloat16 [384, 128, 1024], P('lon', 'lat')
The draws below stay inside these ranges and needn't reach their ends.
Inputs may be any that keep to these rules, and one draw needn't show every extreme that they name: `query_local`: entries of the neighbourhood queries and keys. `key_local`: entries of the neighbourhood queries and keys.
All inputs are finite; a program needn't handle non-finite values.
Results may differ from the reference program's by a relative error of at most 0.015.
Values may be sent and summed in bfloat16 or wider, within the bound.
No kernel may reach another device: no remote copies, remote signals or barrier semaphores. Data moves between devices by JAX's collectives and lax.ppermute only.
A program may use at most 64 MiB of HBM per device.

```python
import math
import jax
import jax.numpy as jnp
from jax import lax

D = 1024
HEADS = 16
TLON = 12
TLAT = 8
RADIUS = 6
WINDOW = 13
STEPS = 4
NLON = 384
NLAT = 128
N_LON = 32
N_LAT = 16


def make_pair(key):
    shape = (NLON, NLAT, D)
    query_key = jax.random.fold_in(key, 11)
    keys_key = jax.random.fold_in(key, 12)
    query = jnp.clip(jax.random.normal(query_key, shape, jnp.float32), -6.0, 6.0)
    keys = jnp.clip(jax.random.normal(keys_key, shape, jnp.float32), -6.0, 6.0)
    return (query, keys)


def draw_query_local(key, part):
    return make_pair(key)[0].astype(jnp.bfloat16)


def draw_key_local(key, part):
    return make_pair(key)[1].astype(jnp.bfloat16)


def draw_tokens(key, part):
    shape = (NLON, NLAT, D)
    values = jax.random.normal(jax.random.fold_in(key, 34), shape, jnp.float32)
    return jnp.clip(values, -6.0, 6.0).astype(jnp.bfloat16)


def draw_global_weight(key, part):
    shape = (D, 3 * D)
    spread = 1.0 / D ** 0.5
    values = jnp.clip(jax.random.normal(jax.random.fold_in(key, 42), shape, jnp.float32), -6.0, 6.0) * spread
    return jnp.clip(values, -1.0, 1.0).astype(jnp.bfloat16)


def level_of(stream_key, extent, split, least, high):
    level, own = 1.0, jax.random.fold_in(stream_key, 6)
    for axis_at, parts in split:
        heights = jnp.exp(jax.random.uniform(jax.random.fold_in(own, axis_at), (parts,), jnp.float32, least / len(split), high / len(split)))
        level = level * jnp.repeat(heights, extent[axis_at] // parts).reshape([-1 if axis == axis_at else 1 for axis in range(len(extent))])
    return level


def centred(key, shape, scale, most, shards=(), held_as=jnp.bfloat16):
    values = scale * jax.random.normal(key, shape, jnp.float32)
    if shards:
        values = values * level_of(key, shape, shards, -0.22, 0.18)
    return jnp.clip(values, -most, most).astype(held_as)


def setup_inputs(seed: int = 0) -> dict:
    splits = jax.random.split(jax.random.key(seed), 9)
    return {
        "tokens": draw_tokens(jax.random.fold_in(splits[8], 71), 0),
        "query_local": draw_query_local(jax.random.fold_in(splits[8], 71), 0),
        "key_local": draw_key_local(jax.random.fold_in(splits[8], 71), 0),
        "value_local": centred(splits[3], (NLON, NLAT, D), 1.0, 6.0, ((0, 32), (1, 16))),
        "position_bias": centred(splits[4], (HEADS, WINDOW, WINDOW), 1.0, 4.0, (), jnp.float32),
        "output_weight": centred(splits[5], (D, D), D ** -0.5, 0.1875, ((0, 16),)),
        "norm_gain": jnp.clip(1.0 + 0.18 * jax.random.normal(splits[6], (D,), jnp.float32), 0.1, 1.9),
        "global_weight": draw_global_weight(jax.random.fold_in(splits[8], 71), 0),
    }


def neighbour_layer(query_local, key_local, value_local, position_bias):
    head_size = D // HEADS
    score_scale = 1.0 / math.sqrt(head_size)
    padded_key = jnp.pad(key_local, ((0, 0), (RADIUS, RADIUS), (0, 0)))
    padded_value = jnp.pad(value_local, ((0, 0), (RADIUS, RADIUS), (0, 0)))
    lat_index = jnp.arange(NLAT + 2 * RADIUS, dtype=jnp.int32) - RADIUS
    lat_inside = (lat_index >= 0) & (lat_index < NLAT)

    def one_block(row_start):
        source_rows = (row_start + jnp.arange(TLON + 2 * RADIUS, dtype=jnp.int32) - RADIUS) % NLON
        key_slab = jnp.take(padded_key, source_rows, axis=0).astype(jnp.float32)
        value_slab = jnp.take(padded_value, source_rows, axis=0).astype(jnp.float32)
        query_block = lax.dynamic_slice_in_dim(query_local, row_start, TLON, 0).astype(jnp.float32)
        query_block = query_block.reshape(TLON, NLAT, HEADS, head_size)
        score_list = []
        for lon_offset in range(WINDOW):
            for lat_offset in range(WINDOW):
                key_part = key_slab[lon_offset:lon_offset + TLON, lat_offset:lat_offset + NLAT]
                key_part = key_part.reshape(TLON, NLAT, HEADS, head_size)
                score_one = jnp.einsum('abhd,abhd->abh', query_block, key_part) * score_scale
                score_one = score_one + position_bias[:, lon_offset, lat_offset]
                valid_one = lat_inside[lat_offset:lat_offset + NLAT][None, :, None]
                score_list.append(jnp.where(valid_one, score_one, -1e+30))
        scores = jnp.stack(score_list, axis=-1)
        largest = lax.optimization_barrier(jnp.max(scores, axis=-1, keepdims=True))
        weights = jnp.exp(scores - largest)
        denominator = lax.optimization_barrier(jnp.sum(weights, axis=-1))
        rounded = lax.optimization_barrier(weights.astype(jnp.bfloat16)).astype(jnp.float32)
        accumulated = jnp.zeros((TLON, NLAT, HEADS, head_size), jnp.float32)
        position = 0
        for lon_offset in range(WINDOW):
            for lat_offset in range(WINDOW):
                value_part = value_slab[lon_offset:lon_offset + TLON, lat_offset:lat_offset + NLAT]
                value_part = value_part.reshape(TLON, NLAT, HEADS, head_size)
                accumulated = accumulated + rounded[..., position][..., None] * value_part
                position = position + 1
        result = accumulated / denominator[..., None]
        return result.reshape(TLON, NLAT, D).astype(jnp.bfloat16)
    starts = jnp.arange(N_LON, dtype=jnp.int32) * TLON
    blocks_out = lax.map(one_block, starts)
    return blocks_out.reshape(NLON, NLAT, D)

def to_blocks(array):
    channels = array.shape[-1]
    shaped = array.reshape(N_LON, TLON, N_LAT, TLAT, channels).transpose(0, 2, 1, 3, 4)
    return shaped.reshape(N_LON * N_LAT, TLON * TLAT, channels)

def from_blocks(array):
    channels = array.shape[-1]
    shaped = array.reshape(N_LON, N_LAT, TLON, TLAT, channels).transpose(0, 2, 1, 3, 4)
    return shaped.reshape(NLON, NLAT, channels)

def reference(tokens, query_local, key_local, value_local, position_bias, output_weight, norm_gain, global_weight):
    head_size = D // HEADS
    score_scale = 1.0 / math.sqrt(head_size)
    local_out = neighbour_layer(query_local, key_local, value_local, position_bias)
    flat_local = local_out.reshape(NLON * NLAT, D)
    projected = jnp.dot(flat_local, output_weight, preferred_element_type=jnp.float32)
    hidden = (tokens.reshape(NLON * NLAT, D).astype(jnp.float32) + projected).astype(jnp.bfloat16)
    widened = hidden.astype(jnp.float32)
    inverse = lax.rsqrt(lax.optimization_barrier(jnp.mean(widened * widened, axis=1, keepdims=True)) + 1e-06)
    normed = (widened * inverse * norm_gain.astype(jnp.float32)).astype(jnp.bfloat16)
    triple = jnp.dot(normed, global_weight, preferred_element_type=jnp.float32).astype(jnp.bfloat16)
    grid_triple = triple.reshape(NLON, NLAT, 3 * D)
    query_blocks = to_blocks(grid_triple[:, :, :D])
    key_blocks = to_blocks(grid_triple[:, :, D:2 * D])
    value_blocks = to_blocks(grid_triple[:, :, 2 * D:])
    block_count = N_LON * N_LAT

    def attend_block(block_index):
        sources = (block_index - jnp.arange(STEPS + 1, dtype=jnp.int32)) % block_count
        keys_near = jnp.take(key_blocks, sources, axis=0).reshape(-1, HEADS, head_size).astype(jnp.float32)
        values_near = jnp.take(value_blocks, sources, axis=0).reshape(-1, HEADS, head_size).astype(jnp.float32)
        query_here = lax.dynamic_index_in_dim(query_blocks, block_index, 0, keepdims=False)
        query_here = query_here.reshape(-1, HEADS, head_size).astype(jnp.float32)
        scores = jnp.einsum('qhd,khd->hqk', query_here, keys_near) * score_scale
        largest = lax.optimization_barrier(jnp.max(scores, axis=2, keepdims=True))
        weights = jnp.exp(scores - largest)
        denominator = lax.optimization_barrier(jnp.sum(weights, axis=2))
        rounded = lax.optimization_barrier(weights.astype(jnp.bfloat16)).astype(jnp.float32)
        weighted = jnp.einsum('hqk,khd->qhd', rounded, values_near)
        result = weighted / jnp.transpose(denominator)[:, :, None]
        return result.reshape(-1, D).astype(jnp.bfloat16)
    attended_blocks = lax.map(attend_block, jnp.arange(block_count, dtype=jnp.int32))
    attended = from_blocks(attended_blocks)
    return (hidden.reshape(NLON, NLAT, D), attended)
```

```python
import functools
import math

import jax
import jax.numpy as jnp
from jax import lax
from jax.experimental import pallas as pl
from jax.experimental.pallas import tpu as pltpu
from jax.sharding import Mesh, PartitionSpec as P

LON = ("zl", "y", "c")
LAT = ("zh", "x")
RADIUS = 6
WINDOW = 13
TL = 12
TJ = 8
CELLS = TL * TJ
HALF = 40
KEYS = 512
NEG = -1e30
VMEM = 48 * 1024 * 1024


def params():
    return pltpu.CompilerParams(vmem_limit_bytes=VMEM)


def vspec():
    return pl.BlockSpec(memory_space=pltpu.VMEM)


def anyspec():
    return pl.BlockSpec(memory_space=pl.ANY)


def sspec():
    return pl.BlockSpec(memory_space=pltpu.SMEM)


def edge_kernel(k_hbm, v_hbm, up_ref, down_ref, buf, sems):
    copies = [pltpu.make_async_copy(ref, buf.at[at], sems.at[at]) for at, ref in enumerate((k_hbm, v_hbm))]
    for copy in copies:
        copy.start()
    row = lax.broadcasted_iota(jnp.int32, (2 * HALF, CELLS), 0)
    col = lax.broadcasted_iota(jnp.int32, (2 * HALF, CELLS), 1)
    half = jnp.where(row >= HALF, 1, 0)
    r = row - half * HALF
    lon = half * 6 + r // 6
    lat = r % 6
    real = r < 36
    first = (real & (col == lon * TJ + lat)).astype(jnp.float32).astype(jnp.bfloat16)
    last = (real & (col == lon * TJ + lat + 2)).astype(jnp.float32).astype(jnp.bfloat16)
    for at, copy in enumerate(copies):
        copy.wait()
        x = buf[at]
        up_ref[at] = jnp.dot(last, x, preferred_element_type=jnp.float32).astype(jnp.bfloat16)
        down_ref[at] = jnp.dot(first, x, preferred_element_type=jnp.float32).astype(jnp.bfloat16)


def edges(k, v):
    shape = jax.ShapeDtypeStruct((2, 2 * HALF, k.shape[1]), jnp.bfloat16)
    return pl.pallas_call(
        edge_kernel,
        out_shape=(shape, shape),
        in_specs=[anyspec()] * 2,
        out_specs=(vspec(), vspec()),
        scratch_shapes=[pltpu.VMEM((2,) + k.shape, jnp.bfloat16), pltpu.SemaphoreType.DMA((2,))],
        compiler_params=params(),
        name="edges",
    )(k, v)


def side_kernel(low_ref, high_ref, k_ref, v_ref, east_ref, west_ref, rows):
    row = lax.broadcasted_iota(jnp.int32, (128, 256), 0)
    col = lax.broadcasted_iota(jnp.int32, (128, 256), 1)
    low = row < HALF
    own = (row >= HALF) & (row < HALF + 48)
    first = jnp.where(low, row, jnp.where(own, 80 + row - HALF, 176 + row - HALF - 48))
    last = jnp.where(own, first + 48, first + HALF)
    pick_first = jnp.where(col == first, 1.0, 0.0).astype(jnp.bfloat16)
    pick_last = jnp.where(col == last, 1.0, 0.0).astype(jnp.bfloat16)
    for at, ref in enumerate((k_ref, v_ref)):
        rows[0:80] = low_ref[at]
        rows[80:176] = ref[...]
        rows[176:256] = high_ref[at]
        x = rows[...]
        east_ref[at] = jnp.dot(pick_last, x, preferred_element_type=jnp.float32).astype(jnp.bfloat16)
        west_ref[at] = jnp.dot(pick_first, x, preferred_element_type=jnp.float32).astype(jnp.bfloat16)


def sides(low, high, k, v):
    shape = jax.ShapeDtypeStruct((2, 128, k.shape[1]), jnp.bfloat16)
    return pl.pallas_call(
        side_kernel,
        out_shape=(shape, shape),
        in_specs=[vspec()] * 4,
        out_specs=(vspec(), vspec()),
        scratch_shapes=[pltpu.VMEM((256, k.shape[1]), jnp.bfloat16)],
        compiler_params=params(),
        name="sides",
    )(low, high, k, v)


def key_places(shape, dim):
    col = lax.broadcasted_iota(jnp.int32, shape, dim)
    lon = 6 + col // TJ
    lat = 6 + col % TJ
    side = jnp.zeros_like(col)

    def halo(base, first_lon, lat_base, which, lon, lat, side):
        r = col - base
        here = (r >= 0) & (r < HALF)
        rr = jnp.clip(r, 0, HALF - 1)
        lon = jnp.where(here, first_lon + rr // 6, lon)
        lat = jnp.where(here, lat_base + rr % 6, lat)
        side = jnp.where(here, jnp.where(rr < 36, which, 3), side)
        return lon, lat, side

    for base, first_lon, lat_base, which in (
        (96, 6, 0, 1),
        (136, 12, 0, 1),
        (176, 6, 14, 2),
        (216, 12, 14, 2),
        (256, 0, 0, 1),
        (344, 0, 14, 2),
        (384, 18, 0, 1),
        (472, 18, 14, 2),
    ):
        lon, lat, side = halo(base, first_lon, lat_base, which, lon, lat, side)
    for base, first_lon in ((296, 0), (424, 18)):
        r = col - base
        here = (r >= 0) & (r < 48)
        rr = jnp.clip(r, 0, 47)
        lon = jnp.where(here, first_lon + rr // TJ, lon)
        lat = jnp.where(here, 6 + rr % TJ, lat)
        side = jnp.where(here, 0, side)
    return lon, lat, side


def bias_kernel(place_ref, table_ref, out_ref):
    heads = out_ref.shape[0]
    rows = heads * TJ
    table = jnp.broadcast_to(table_ref[...][:, None, :], (heads, TJ, 256)).reshape(rows, 256)
    high = table.astype(jnp.bfloat16).astype(jnp.float32)
    mid = (table - high).astype(jnp.bfloat16).astype(jnp.float32)
    low = table - high - mid
    parts = jnp.concatenate([high, mid, low], axis=0)
    lat_of_row = lax.broadcasted_iota(jnp.int32, parts.shape, 0) % TJ
    index = lax.broadcasted_iota(jnp.int32, (256, 384), 0)
    column = lax.broadcasted_iota(jnp.int32, (1, 384), 1)
    lon_gap, key_lat = column // 20, column % 20
    strip = jnp.zeros((3 * rows, 384), jnp.float32)
    for j in range(TJ):
        here = jnp.where(lat_of_row == j, parts, 0.0).astype(jnp.bfloat16)
        fits = (key_lat >= j) & (key_lat < j + WINDOW) & (lon_gap < WINDOW)
        wanted = jnp.where(fits, lon_gap * WINDOW + key_lat - j, -1)
        hot = jnp.where(index == wanted, 1.0, 0.0).astype(jnp.bfloat16)
        strip += jnp.dot(here, hot, preferred_element_type=jnp.float32)
    strip = strip.astype(jnp.bfloat16)
    strip = jnp.concatenate([strip[:rows], strip[rows : 2 * rows], strip[2 * rows :]], axis=1)

    lon, lat, side = key_places((1, KEYS), 1)
    at_south = place_ref[3] == 0
    at_north = place_ref[3] == place_ref[4] - 1
    closed = (side == 3) | ((side == 1) & at_south) | ((side == 2) & at_north)
    row = lax.broadcasted_iota(jnp.int32, (384, KEYS), 0)
    lat_gap = lat - lax.broadcasted_iota(jnp.int32, (TJ, KEYS), 0)
    near = (lat_gap >= 0) & (lat_gap < WINDOW) & jnp.logical_not(closed)
    for i in range(TL):
        gap = lon - i
        inside = (gap >= 0) & (gap < WINDOW)
        hot = jnp.where(row == jnp.where(inside, gap * 20 + lat, -1), 1.0, 0.0).astype(jnp.bfloat16)
        hot = jnp.concatenate([hot, hot, hot], axis=0)
        found = jnp.dot(strip, hot, preferred_element_type=jnp.float32)
        found = jnp.where((near & inside)[None], found.reshape(heads, TJ, KEYS), NEG)
        out_ref[:, TJ * i : TJ * i + TJ, :] = found


def bias_table(position_bias, place):
    heads = position_bias.shape[0]
    table = position_bias.reshape(heads, WINDOW * WINDOW)
    table = jnp.pad(table, ((0, 0), (0, 256 - WINDOW * WINDOW)))
    return pl.pallas_call(
        bias_kernel,
        out_shape=jax.ShapeDtypeStruct((heads, CELLS, KEYS), jnp.float32),
        in_specs=[sspec(), vspec()],
        out_specs=vspec(),
        compiler_params=params(),
        name="bias",
    )(place, table)


def pair_attention(q, k, v, bias):
    n = q.shape[0]
    lane = lax.broadcasted_iota(jnp.int32, (n, 128), 1)
    zero = jnp.zeros_like(q)
    both = jnp.concatenate([jnp.where(lane < 64, q, zero), jnp.where(lane >= 64, q, zero)], axis=0)
    scores = lax.dot_general(both, k, (((1,), (1,)), ((), ())), preferred_element_type=jnp.float32)
    if bias is not None:
        scores = scores + bias
    largest = jnp.max(scores, axis=1, keepdims=True)
    weights = jnp.exp(scores - largest)
    total = jnp.sum(weights, axis=1, keepdims=True)
    out = jnp.dot(weights.astype(jnp.bfloat16), v, preferred_element_type=jnp.float32) / total
    return jnp.where(lane < 64, out[:n], out[n:]).astype(jnp.bfloat16)


def attend_kernel(
    q_ref, k_ref, v_ref, low_ref, high_ref, west_ref, east_ref, bias_ref, out_ref, kbuf, vbuf
):
    width = q_ref.shape[1]
    for buf, own, at in ((kbuf, k_ref, 0), (vbuf, v_ref, 1)):
        buf[0:96] = own[...]
        buf[96:176] = low_ref[at]
        buf[176:256] = high_ref[at]
        buf[256:384] = west_ref[at]
        buf[384:512] = east_ref[at]
    for p in range(width // 128):
        lanes = slice(128 * p, 128 * p + 128)
        q = q_ref[:, lanes] * jnp.bfloat16(0.125)
        bias = bias_ref[2 * p : 2 * p + 2].reshape(2 * CELLS, KEYS)
        out = pair_attention(q, kbuf[:, lanes], vbuf[:, lanes], bias)
        for e in range(2):
            at = turned(2 * p + e) * 64
            out_ref[:, at : at + 64] = out[:, 64 * e : 64 * e + 64]


def turned(chunk):
    return (chunk % 4) * 4 + chunk // 4


def attend(q, k, v, low, high, west, east, bias):
    width = q.shape[1]
    return pl.pallas_call(
        attend_kernel,
        out_shape=jax.ShapeDtypeStruct(q.shape, jnp.bfloat16),
        in_specs=[vspec()] * 8,
        out_specs=vspec(),
        scratch_shapes=[
            pltpu.VMEM((KEYS, width), jnp.bfloat16),
            pltpu.VMEM((KEYS, width), jnp.bfloat16),
        ],
        compiler_params=params(),
        name="local",
    )(q, k, v, low, high, west, east, bias)


def project_kernel(at_ref, x_ref, tok_ref, mine_ref, other_ref, gain_ref, hid_ref, norm_ref, pbuf):
    width = x_ref.shape[1]
    core, xpos = at_ref[0], at_ref[1]
    side = width // 2
    deep = width // 4
    for ref, where in ((mine_ref, core), (other_ref, 1 - core)):
        total = jnp.zeros((CELLS, side), jnp.float32)
        for u in range(4):
            lanes = pl.ds(pl.multiple_of(lax.rem(xpos + u, 4) * deep, deep), deep)
            total += jnp.dot(
                x_ref[:, lanes], ref[deep * u : deep * u + deep], preferred_element_type=jnp.float32
            )
        pbuf[:, pl.ds(pl.multiple_of(where * side, side), side)] = total
    hidden = (tok_ref[...].astype(jnp.float32) + pbuf[...]).astype(jnp.bfloat16)
    hid_ref[...] = hidden
    wide = hidden.astype(jnp.float32)
    inverse = lax.rsqrt(jnp.mean(wide * wide, axis=1, keepdims=True) + 1e-06)
    normed = (wide * inverse * gain_ref[...]).astype(jnp.bfloat16)
    for chunk in range(width // 64):
        at = turned(chunk) * 64
        norm_ref[:, at : at + 64] = normed[:, 64 * chunk : 64 * chunk + 64]


def project(at, x, tok, mine, other, gain):
    shape = jax.ShapeDtypeStruct(x.shape, jnp.bfloat16)
    return pl.pallas_call(
        project_kernel,
        out_shape=(shape, shape),
        in_specs=[sspec()] + [vspec()] * 5,
        out_specs=(vspec(), vspec()),
        scratch_shapes=[pltpu.VMEM(x.shape, jnp.float32)],
        compiler_params=params(),
        name="project",
    )(at, x, tok, mine, other, gain)


def global_kernel(side_ref, x0, x1, x2, x3, x4, wq, wk, wv, *rest):
    out_ref, xbuf = rest[-2:]

    @pl.when(pl.program_id(0) == 0)
    def _():
        for at, ref in enumerate((x0, x1, x2, x3, x4)):
            xbuf[CELLS * at : CELLS * at + CELLS] = ref[...]

    def part(rows, w):
        return jnp.dot(rows, w[...], preferred_element_type=jnp.float32).astype(jnp.bfloat16)

    q = part(xbuf[0:CELLS], wq) * jnp.bfloat16(0.125)
    k = part(xbuf[...], wk)
    v = part(xbuf[...], wv)
    for p in range(q.shape[1] // 128):
        lanes = slice(128 * p, 128 * p + 128)
        out_ref[:, lanes] = pair_attention(q[:, lanes], k[:, lanes], v[:, lanes], None)


def global_layer(side, blocks, weights, before):
    cells, width = blocks[0].shape
    whole = pl.BlockSpec((cells, width), lambda g, c: (0, 0))
    weight = [pl.BlockSpec((width, 256), lambda g, c, t=t: (0, 2 * t + g)) for t in range(3)]
    more = [] if before is None else [before]
    return pl.pallas_call(
        global_kernel,
        out_shape=jax.ShapeDtypeStruct((cells, width), jnp.bfloat16),
        grid_spec=pltpu.PrefetchScalarGridSpec(
            num_scalar_prefetch=1,
            grid=(2,),
            in_specs=[whole] * 5 + weight + [pl.BlockSpec(memory_space=pl.ANY)] * len(more),
            out_specs=pl.BlockSpec((cells, 256), lambda g, c: (0, 2 * c[0] + g)),
            scratch_shapes=[pltpu.VMEM((5 * cells, width), jnp.bfloat16)],
        ),
        input_output_aliases={9: 0} if more else {},
        compiler_params=params(),
        name="global",
    )(side, *blocks, weights, weights, weights, *more)


def pick_kernel(at_ref, o_ref, g_ref, half_ref, again_ref, sems):
    core = at_ref[0]
    side = half_ref.shape[1] // 4
    copies = []
    for t in range(4):
        ref, first = (o_ref, 0) if t == 0 else (g_ref, 2 * side * (t - 1))
        lanes = pl.ds(pl.multiple_of(first + core * side, side), side)
        to = half_ref.at[:, pl.ds(side * t, side)]
        copies.append(pltpu.make_async_copy(ref.at[:, lanes], to, sems.at[t]))
    for copy in copies:
        copy.start()
    for i in range(at_ref.shape[0]):
        again_ref[i] = at_ref[i]
    for copy in copies:
        copy.wait()


def pick(at, o, g):
    rows, columns = o.shape[0], (o.shape[1] + g.shape[1]) // 2
    return pl.pallas_call(
        pick_kernel,
        out_shape=[jax.ShapeDtypeStruct((rows, columns), o.dtype), jax.ShapeDtypeStruct(at.shape, at.dtype)],
        in_specs=[sspec(), anyspec(), anyspec()],
        out_specs=[vspec(), sspec()],
        scratch_shapes=[pltpu.SemaphoreType.DMA((4,))],
        compiler_params=params(),
        name="pick",
    )(at, o, g)


def place_kernel(at_ref, p0, p1, p2, p3, *rest):
    out_o, out_g = rest[-2:]
    rows, side = p0.shape[0], out_o.shape[1]
    for u, ref in enumerate((p0, p1, p2, p3)):
        to = pl.ds(pl.multiple_of(lax.rem(at_ref[2] + u, 4) * rows, rows), rows)
        out_o[to] = ref[:, :side]
        out_g[to] = ref[:, side:]


def place_rows(at, pieces, after):
    rows, columns = pieces[0].shape
    shapes = [jax.ShapeDtypeStruct((rows * 4, c), pieces[0].dtype) for c in (columns // 4, columns * 3 // 4)]
    return pl.pallas_call(
        place_kernel,
        out_shape=shapes,
        in_specs=[sspec()] + [vspec()] * len(pieces) + [anyspec()] * len(after),
        out_specs=[vspec(), vspec()],
        compiler_params=params(),
        name="place",
    )(at, *pieces, *after)


def join_kernel(p0, p1, p2, p3, *rest):
    out_ref = rest[-1]
    rows = p0.shape[0]
    for u, ref in enumerate((p0, p1, p2, p3)):
        out_ref[rows * u : rows * u + rows] = ref[...]


def join(pieces, after):
    rows, columns = pieces[0].shape
    return pl.pallas_call(
        join_kernel,
        out_shape=jax.ShapeDtypeStruct((rows * len(pieces), columns), pieces[0].dtype),
        in_specs=[vspec()] * len(pieces) + [anyspec()] * len(after),
        out_specs=vspec(),
        compiler_params=params(),
        name="join",
    )(*pieces, *after)


def ring(count, by):
    return [(i, (i + by) % count) for i in range(count)]


def body(tokens, query_local, key_local, value_local, position_bias, output_weight, norm_gain, global_weight):
    width = tokens.shape[2]
    half = width // 2
    flat = lambda a: a.reshape(CELLS, width)
    q, k, v, tok = flat(query_local), flat(key_local), flat(value_local), flat(tokens)
    core = lax.axis_index("c")
    lat = lax.axis_index(LAT)
    lat_count = lax.axis_size(LAT)
    lon_count = lax.axis_size(LON)
    xs, zs = lax.axis_size("x"), lax.axis_size("zh")
    x, zh = lax.axis_index("x"), lax.axis_index("zh")
    at = jnp.stack([core, x, zh, lat, jnp.int32(lat_count)]).astype(jnp.int32)
    swap = [(0, 1), (1, 0)]

    up, down = edges(k, v)
    low = lax.ppermute(up, LAT, [(i, i + 1) for i in range(lat_count - 1)])
    high = lax.ppermute(down, LAT, [(i + 1, i) for i in range(lat_count - 1)])
    columns, at = pick(at, output_weight, global_weight)
    pieces = [columns] + [lax.ppermute(columns, "zh", ring(zs, -by)) for by in range(1, zs)]
    bias = bias_table(position_bias, at)

    to_east, to_west = sides(low, high, k, v)
    west = lax.ppermute(to_east, LON, ring(lon_count, 1))
    east = lax.ppermute(to_west, LON, ring(lon_count, -1))

    rows_o, rows_g = place_rows(at, pieces, [bias, to_east, to_west])
    pieces = [rows_o] + [lax.ppermute(rows_o, "x", ring(xs, -by)) for by in range(1, xs)]
    mine_o = join(pieces, [west, east])
    other_o = lax.ppermute(mine_o, "c", swap)
    mine_g = lax.all_gather(rows_g, "x", axis=0, tiled=True)

    local_out = attend(q, k, v, low, high, west, east, bias)
    hidden, normed = project(at, local_out, tok, mine_o, other_o, norm_gain.reshape(1, width))
    behind = lax.ppermute(normed, LON + ("zh",), ring(lon_count * zs, 1))
    blocks = [normed]
    for by in range(1, xs):
        sent = jnp.where(x + by < xs, normed, behind)
        blocks.append(lax.ppermute(sent, "x", ring(xs, by)))
    blocks.append(behind)
    mine_g, *blocks = lax.optimization_barrier((mine_g, *blocks))
    other_g = lax.ppermute(mine_g, "c", swap)
    attended = global_layer(at[:1], blocks, mine_g, None)
    attended = global_layer(1 - at[:1], blocks, other_g, attended)
    return hidden.reshape(tokens.shape), attended.reshape(tokens.shape)


def solution(mesh):
    fine = Mesh(mesh.devices.reshape(2, 8, 2, 4, 4), LON + LAT)
    grid = P(LON, LAT, None)
    return jax.shard_map(
        body,
        mesh=fine,
        in_specs=(grid, grid, grid, grid, P(), P(LAT, None), P(), P(LAT, None)),
        out_specs=(grid, grid),
        check_vma=False,
    )
```

```python
import functools
import math

import jax
import jax.numpy as jnp
from jax import lax
from jax.experimental import pallas as pl
from jax.experimental.pallas import tpu as pltpu
from jax.sharding import Mesh, PartitionSpec as P

LON = ("zl", "y", "c")
LAT = ("zh", "x")
RADIUS = 6
WINDOW = 13
TL = 12
TJ = 8
CELLS = TL * TJ
HALF = 40
KEYS = 512
NEG = -1e30
MIB = 1024 * 1024


def params(mib):
    return pltpu.CompilerParams(vmem_limit_bytes=mib * MIB)


def vspec():
    return pl.BlockSpec(memory_space=pltpu.VMEM)


def anyspec():
    return pl.BlockSpec(memory_space=pl.ANY)


def sspec():
    return pl.BlockSpec(memory_space=pltpu.SMEM)


def edge_kernel(k_hbm, v_hbm, up_ref, down_ref, buf, sems):
    copies = [pltpu.make_async_copy(ref, buf.at[at], sems.at[at]) for at, ref in enumerate((k_hbm, v_hbm))]
    for copy in copies:
        copy.start()
    row = lax.broadcasted_iota(jnp.int32, (2 * HALF, CELLS), 0)
    col = lax.broadcasted_iota(jnp.int32, (2 * HALF, CELLS), 1)
    half = jnp.where(row >= HALF, 1, 0)
    r = row - half * HALF
    lon = half * 6 + r // 6
    lat = r % 6
    real = r < 36
    first = (real & (col == lon * TJ + lat)).astype(jnp.float32).astype(jnp.bfloat16)
    last = (real & (col == lon * TJ + lat + 2)).astype(jnp.float32).astype(jnp.bfloat16)
    for at, copy in enumerate(copies):
        copy.wait()
        x = buf[at]
        up_ref[at] = jnp.dot(last, x, preferred_element_type=jnp.float32).astype(jnp.bfloat16)
        down_ref[at] = jnp.dot(first, x, preferred_element_type=jnp.float32).astype(jnp.bfloat16)


def edges(k, v):
    shape = jax.ShapeDtypeStruct((2, 2 * HALF, k.shape[1]), jnp.bfloat16)
    return pl.pallas_call(
        edge_kernel,
        out_shape=(shape, shape),
        in_specs=[anyspec()] * 2,
        out_specs=(vspec(), vspec()),
        scratch_shapes=[pltpu.VMEM((2,) + k.shape, jnp.bfloat16), pltpu.SemaphoreType.DMA((2,))],
        compiler_params=params(6),
        name="edges",
    )(k, v)


def side_kernel(low_ref, high_ref, k_ref, v_ref, after_ref, east_ref, west_ref, rows):
    row = lax.broadcasted_iota(jnp.int32, (128, 256), 0)
    col = lax.broadcasted_iota(jnp.int32, (128, 256), 1)
    low = row < HALF
    own = (row >= HALF) & (row < HALF + 48)
    first = jnp.where(low, row, jnp.where(own, 80 + row - HALF, 176 + row - HALF - 48))
    last = jnp.where(own, first + 48, first + HALF)
    pick_first = jnp.where(col == first, 1.0, 0.0).astype(jnp.bfloat16)
    pick_last = jnp.where(col == last, 1.0, 0.0).astype(jnp.bfloat16)
    for at, ref in enumerate((k_ref, v_ref)):
        rows[0:80] = low_ref[at]
        rows[80:176] = ref[...]
        rows[176:256] = high_ref[at]
        x = rows[...]
        east_ref[at] = jnp.dot(pick_last, x, preferred_element_type=jnp.float32).astype(jnp.bfloat16)
        west_ref[at] = jnp.dot(pick_first, x, preferred_element_type=jnp.float32).astype(jnp.bfloat16)


def sides(low, high, k, v, after):
    shape = jax.ShapeDtypeStruct((2, 128, k.shape[1]), jnp.bfloat16)
    return pl.pallas_call(
        side_kernel,
        out_shape=(shape, shape),
        in_specs=[vspec()] * 4 + [anyspec()],
        out_specs=(vspec(), vspec()),
        scratch_shapes=[pltpu.VMEM((256, k.shape[1]), jnp.bfloat16)],
        compiler_params=params(6),
        name="sides",
    )(low, high, k, v, after)


def key_places(shape, dim):
    col = lax.broadcasted_iota(jnp.int32, shape, dim)
    lon = 6 + col // TJ
    lat = 6 + col % TJ
    side = jnp.zeros_like(col)

    def halo(base, first_lon, lat_base, which, lon, lat, side):
        r = col - base
        here = (r >= 0) & (r < HALF)
        rr = jnp.clip(r, 0, HALF - 1)
        lon = jnp.where(here, first_lon + rr // 6, lon)
        lat = jnp.where(here, lat_base + rr % 6, lat)
        side = jnp.where(here, jnp.where(rr < 36, which, 3), side)
        return lon, lat, side

    for base, first_lon, lat_base, which in (
        (96, 6, 0, 1),
        (136, 12, 0, 1),
        (176, 6, 14, 2),
        (216, 12, 14, 2),
        (256, 0, 0, 1),
        (344, 0, 14, 2),
        (384, 18, 0, 1),
        (472, 18, 14, 2),
    ):
        lon, lat, side = halo(base, first_lon, lat_base, which, lon, lat, side)
    for base, first_lon in ((296, 0), (424, 18)):
        r = col - base
        here = (r >= 0) & (r < 48)
        rr = jnp.clip(r, 0, 47)
        lon = jnp.where(here, first_lon + rr // TJ, lon)
        lat = jnp.where(here, 6 + rr % TJ, lat)
        side = jnp.where(here, 0, side)
    return lon, lat, side


def bias_kernel(place_ref, table_ref, out_ref):
    heads = out_ref.shape[0]
    rows = heads * TJ
    table = jnp.broadcast_to(table_ref[...][:, None, :], (heads, TJ, 256)).reshape(rows, 256)
    high = table.astype(jnp.bfloat16).astype(jnp.float32)
    mid = (table - high).astype(jnp.bfloat16).astype(jnp.float32)
    low = table - high - mid
    parts = jnp.concatenate([high, mid, low], axis=0)
    lat_of_row = lax.broadcasted_iota(jnp.int32, parts.shape, 0) % TJ
    index = lax.broadcasted_iota(jnp.int32, (256, 384), 0)
    column = lax.broadcasted_iota(jnp.int32, (1, 384), 1)
    lon_gap, key_lat = column // 20, column % 20
    strip = jnp.zeros((3 * rows, 384), jnp.float32)
    for j in range(TJ):
        here = jnp.where(lat_of_row == j, parts, 0.0).astype(jnp.bfloat16)
        fits = (key_lat >= j) & (key_lat < j + WINDOW) & (lon_gap < WINDOW)
        wanted = jnp.where(fits, lon_gap * WINDOW + key_lat - j, -1)
        hot = jnp.where(index == wanted, 1.0, 0.0).astype(jnp.bfloat16)
        strip += jnp.dot(here, hot, preferred_element_type=jnp.float32)
    strip = strip.astype(jnp.bfloat16)
    strip = jnp.concatenate([strip[:rows], strip[rows : 2 * rows], strip[2 * rows :]], axis=1)

    lon, lat, side = key_places((1, KEYS), 1)
    at_south = place_ref[3] == 0
    at_north = place_ref[3] == place_ref[4] - 1
    closed = (side == 3) | ((side == 1) & at_south) | ((side == 2) & at_north)
    row = lax.broadcasted_iota(jnp.int32, (384, KEYS), 0)
    lat_gap = lat - lax.broadcasted_iota(jnp.int32, (TJ, KEYS), 0)
    near = (lat_gap >= 0) & (lat_gap < WINDOW) & jnp.logical_not(closed)
    for i in range(TL):
        gap = lon - i
        inside = (gap >= 0) & (gap < WINDOW)
        hot = jnp.where(row == jnp.where(inside, gap * 20 + lat, -1), 1.0, 0.0).astype(jnp.bfloat16)
        hot = jnp.concatenate([hot, hot, hot], axis=0)
        found = jnp.dot(strip, hot, preferred_element_type=jnp.float32)
        found = jnp.where((near & inside)[None], found.reshape(heads, TJ, KEYS), NEG)
        out_ref[:, TJ * i : TJ * i + TJ, :] = found


def bias_table(position_bias, place):
    heads = position_bias.shape[0]
    table = position_bias.reshape(heads, WINDOW * WINDOW)
    table = jnp.pad(table, ((0, 0), (0, 256 - WINDOW * WINDOW)))
    return pl.pallas_call(
        bias_kernel,
        out_shape=jax.ShapeDtypeStruct((heads, CELLS, KEYS), jnp.float32),
        in_specs=[sspec(), vspec()],
        out_specs=vspec(),
        compiler_params=params(12),
        name="bias",
    )(place, table)


def pair_attention(q, k, v, bias):
    n = q.shape[0]
    lane = lax.broadcasted_iota(jnp.int32, (n, 128), 1)
    zero = jnp.zeros_like(q)
    both = jnp.concatenate([jnp.where(lane < 64, q, zero), jnp.where(lane >= 64, q, zero)], axis=0)
    scores = lax.dot_general(both, k, (((1,), (1,)), ((), ())), preferred_element_type=jnp.float32)
    if bias is not None:
        scores = scores + bias
    largest = jnp.max(scores, axis=1, keepdims=True)
    weights = jnp.exp(scores - largest)
    total = jnp.sum(weights, axis=1, keepdims=True)
    out = jnp.dot(weights.astype(jnp.bfloat16), v, preferred_element_type=jnp.float32) / total
    return jnp.where(lane < 64, out[:n], out[n:]).astype(jnp.bfloat16)


def attend_kernel(
    q_ref, k_ref, v_ref, low_ref, high_ref, west_ref, east_ref, bias_ref, out_ref, kbuf, vbuf
):
    width = q_ref.shape[1]
    for buf, own, at in ((kbuf, k_ref, 0), (vbuf, v_ref, 1)):
        buf[0:96] = own[...]
        buf[96:176] = low_ref[at]
        buf[176:256] = high_ref[at]
        buf[256:384] = west_ref[at]
        buf[384:512] = east_ref[at]
    for p in range(width // 128):
        lanes = slice(128 * p, 128 * p + 128)
        q = q_ref[:, lanes] * jnp.bfloat16(0.125)
        bias = bias_ref[2 * p : 2 * p + 2].reshape(2 * CELLS, KEYS)
        out = pair_attention(q, kbuf[:, lanes], vbuf[:, lanes], bias)
        for e in range(2):
            at = turned(2 * p + e) * 64
            out_ref[:, at : at + 64] = out[:, 64 * e : 64 * e + 64]


def turned(chunk):
    return (chunk % 4) * 4 + chunk // 4


def attend(q, k, v, low, high, west, east, bias):
    width = q.shape[1]
    return pl.pallas_call(
        attend_kernel,
        out_shape=jax.ShapeDtypeStruct(q.shape, jnp.bfloat16),
        in_specs=[vspec()] * 8,
        out_specs=vspec(),
        scratch_shapes=[
            pltpu.VMEM((KEYS, width), jnp.bfloat16),
            pltpu.VMEM((KEYS, width), jnp.bfloat16),
        ],
        compiler_params=params(16),
        name="local",
    )(q, k, v, low, high, west, east, bias)


def piece_lanes(at_ref, deep):
    core, x = at_ref[0], at_ref[1]
    half = deep // 2
    far = lax.rem(x + 2, 4) * deep
    starts = (
        x * deep,
        lax.rem(x + 3 + 2 * core, 4) * deep,
        lax.rem(x + 5 - 2 * core, 4) * deep,
        far + core * half,
        far + (1 - core) * half,
    )
    return [pl.ds(pl.multiple_of(start, half), deep if n < 3 else half) for n, start in enumerate(starts)]


def project_kernel(at_ref, x_ref, tok_ref, gain_ref, p0, p1, p2, p3, p4, hid_ref, norm_ref):
    width = x_ref.shape[1]
    total = None
    for lanes, ref in zip(piece_lanes(at_ref, width // 4), (p0, p1, p2, p3, p4)):
        term = jnp.dot(x_ref[:, lanes], ref[...], preferred_element_type=jnp.float32)
        total = term if total is None else total + term
    hidden = (tok_ref[...].astype(jnp.float32) + total).astype(jnp.bfloat16)
    hid_ref[...] = hidden
    wide = hidden.astype(jnp.float32)
    inverse = lax.rsqrt(jnp.mean(wide * wide, axis=1, keepdims=True) + 1e-06)
    normed = (wide * inverse * gain_ref[...]).astype(jnp.bfloat16)
    for chunk in range(width // 64):
        at = turned(chunk) * 64
        norm_ref[:, at : at + 64] = normed[:, 64 * chunk : 64 * chunk + 64]


def project(at, x, tok, gain, pieces):
    shape = jax.ShapeDtypeStruct(x.shape, jnp.bfloat16)
    return pl.pallas_call(
        project_kernel,
        out_shape=(shape, shape),
        in_specs=[sspec()] + [vspec()] * (3 + len(pieces)),
        out_specs=(vspec(), vspec()),
        compiler_params=params(8),
        name="project",
    )(at, x, tok, gain, *pieces)


def global_kernel(at_ref, x0, x1, x2, x3, x4, *rest):
    weights, (out_ref, xbuf) = rest[:15], rest[15:]
    width = x0.shape[1]

    @pl.when(pl.program_id(0) == 0)
    def _():
        for at, ref in enumerate((x0, x1, x2, x3, x4)):
            xbuf[CELLS * at : CELLS * at + CELLS] = ref[...]

    spans = piece_lanes(at_ref, width // 4)

    def part(rows, refs):
        total = None
        for lanes, ref in zip(spans, refs):
            term = jnp.dot(xbuf[0:rows, lanes], ref[...], preferred_element_type=jnp.float32)
            total = term if total is None else total + term
        return total.astype(jnp.bfloat16)

    q = part(CELLS, weights[0:5]) * jnp.bfloat16(0.125)
    k = part(5 * CELLS, weights[5:10])
    v = part(5 * CELLS, weights[10:15])
    for p in range(q.shape[1] // 128):
        lanes = slice(128 * p, 128 * p + 128)
        out_ref[:, lanes] = pair_attention(q[:, lanes], k[:, lanes], v[:, lanes], None)


def global_layer(at, blocks, pieces):
    cells, width = blocks[0].shape
    steps = width // 256
    whole = pl.BlockSpec((cells, width), lambda g, c: (0, 0))
    weights = [
        pl.BlockSpec((piece.shape[0], 256), lambda g, c, t=t: (0, steps * t + g)) for t in range(3) for piece in pieces
    ]
    return pl.pallas_call(
        global_kernel,
        out_shape=jax.ShapeDtypeStruct((cells, width), jnp.bfloat16),
        grid_spec=pltpu.PrefetchScalarGridSpec(
            num_scalar_prefetch=1,
            grid=(steps,),
            in_specs=[whole] * 5 + weights,
            out_specs=pl.BlockSpec((cells, 256), lambda g, c: (0, g)),
            scratch_shapes=[pltpu.VMEM((5 * cells, width), jnp.bfloat16)],
        ),
        compiler_params=params(20),
        name="global",
    )(at, *blocks, *(pieces * 3))


def pick_kernel(at_ref, o_ref, g_ref, after_ref, out_ref, again_ref, sems):
    side = o_ref.shape[1]
    copies = [
        pltpu.make_async_copy(o_ref, out_ref.at[:, pl.ds(0, side)], sems.at[0]),
        pltpu.make_async_copy(g_ref, out_ref.at[:, pl.ds(side, g_ref.shape[1])], sems.at[1]),
    ]
    for copy in copies:
        copy.start()
    for i in range(at_ref.shape[0]):
        again_ref[i] = at_ref[i]
    for copy in copies:
        copy.wait()


def pick(at, o, g, after):
    shape = jax.ShapeDtypeStruct((o.shape[0], o.shape[1] + g.shape[1]), o.dtype)
    return pl.pallas_call(
        pick_kernel,
        out_shape=[shape, jax.ShapeDtypeStruct(at.shape, at.dtype)],
        in_specs=[sspec()] + [anyspec()] * 3,
        out_specs=[vspec(), sspec()],
        scratch_shapes=[pltpu.SemaphoreType.DMA((2,))],
        compiler_params=params(4),
        name="pick",
    )(at, o, g, after)


def place_kernel(at_ref, p0, p1, p2, p3, p4, *rest, first):
    out_ref = rest[-1]
    rows, side = p0.shape[0], out_ref.shape[1]
    half = rows // 2
    core, zh = at_ref[0], at_ref[2]
    far = lax.rem(zh + 2, 4) * rows
    starts = (
        zh * rows,
        lax.rem(zh + 3 + 2 * core, 4) * rows,
        lax.rem(zh + 5 - 2 * core, 4) * rows,
        far + core * half,
        far + (1 - core) * half,
    )
    for start, ref in zip(starts, (p0, p1, p2, p3, p4)):
        to = pl.ds(pl.multiple_of(start, half), ref.shape[0])
        out_ref[to] = ref[:, first : first + side]


def place_rows(at, pieces, first, count, after):
    rows = pieces[0].shape[0]
    return pl.pallas_call(
        functools.partial(place_kernel, first=first),
        out_shape=jax.ShapeDtypeStruct((rows * 4, count), pieces[0].dtype),
        in_specs=[sspec()] + [vspec()] * len(pieces) + [anyspec()] * len(after),
        out_specs=vspec(),
        compiler_params=params(8),
        name="place",
    )(at, *pieces, *after)


def half_kernel(at_ref, x_ref, *rest):
    out_ref = rest[-1]
    rows = out_ref.shape[0]
    out_ref[...] = x_ref[pl.ds(pl.multiple_of(at_ref[0] * rows, rows), rows)]


def half_of(at, x, after):
    return pl.pallas_call(
        half_kernel,
        out_shape=jax.ShapeDtypeStruct((x.shape[0] // 2, x.shape[1]), x.dtype),
        in_specs=[sspec(), vspec()] + [anyspec()] * len(after),
        out_specs=vspec(),
        compiler_params=params(8),
        name="half",
    )(at, x, *after)


def gathered(rows, axis, at, after):
    roles = [(i, (i + 1) % 4) for i in range(4)] + [(4 + i, 4 + (i + 3) % 4) for i in range(4)]
    swap = [(0, 1), (1, 0)]
    near = lax.ppermute(rows, ("c", axis), roles)
    far = lax.ppermute(half_of(at, near, after), ("c", axis), roles)
    return [rows, near, lax.ppermute(near, "c", swap), far, lax.ppermute(far, "c", swap)]


def ring(count, by):
    return [(i, (i + by) % count) for i in range(count)]


def body(tokens, query_local, key_local, value_local, position_bias, output_weight, norm_gain, global_weight):
    width = tokens.shape[2]
    flat = lambda a: a.reshape(CELLS, width)
    q, k, v, tok = flat(query_local), flat(key_local), flat(value_local), flat(tokens)
    core = lax.axis_index("c")
    lat = lax.axis_index(LAT)
    lat_count = lax.axis_size(LAT)
    lon_count = lax.axis_size(LON)
    xs, zs = lax.axis_size("x"), lax.axis_size("zh")
    x, zh = lax.axis_index("x"), lax.axis_index("zh")
    at = jnp.stack([core, x, zh, lat, jnp.int32(lat_count)]).astype(jnp.int32)
    up, down = edges(k, v)
    low = lax.ppermute(up, LAT, [(i, i + 1) for i in range(lat_count - 1)])
    high = lax.ppermute(down, LAT, [(i + 1, i) for i in range(lat_count - 1)])
    weights, at = pick(at, output_weight, global_weight, up)
    bias = bias_table(position_bias, at)
    to_east, to_west = sides(low, high, k, v, bias)
    west = lax.ppermute(to_east, LON, ring(lon_count, 1))
    east = lax.ppermute(to_west, LON, ring(lon_count, -1))
    pieces = gathered(weights, "zh", at, [])
    rows_o = place_rows(at, pieces, 0, width, [west, east])
    pieces_o = gathered(rows_o, "x", at, [])
    local_out = attend(q, k, v, low, high, west, east, bias)
    rows_g = place_rows(at, pieces, width, 3 * width, [pieces_o[1], local_out])
    hidden, normed = project(at, local_out, tok, norm_gain.reshape(1, width), pieces_o)
    behind = lax.ppermute(normed, LON + ("zh",), ring(lon_count * zs, 1))
    pieces_g = gathered(rows_g, "x", at, [behind])
    blocks = [normed]
    for by in range(1, xs):
        sent = jnp.where(x + by < xs, normed, behind)
        blocks.append(lax.ppermute(sent, "x", ring(xs, by)))
    blocks.append(behind)
    attended = global_layer(at, blocks, pieces_g)
    return hidden.reshape(tokens.shape), attended.reshape(tokens.shape)


def solution(mesh):
    fine = Mesh(mesh.devices.reshape(2, 8, 2, 4, 4), LON + LAT)
    grid = P(LON, LAT, None)
    return jax.shard_map(
        body,
        mesh=fine,
        in_specs=(grid, grid, grid, grid, P(), P(LAT, None), P(), P(LAT, None)),
        out_specs=(grid, grid),
        check_vma=False,
    )
```

```python
import functools
import math

import jax
import jax.numpy as jnp
from jax import lax
from jax.experimental import pallas as pl
from jax.experimental.pallas import tpu as pltpu
from jax.sharding import Mesh, PartitionSpec as P

LON = ("zl", "y", "c")
LAT = ("zh", "x")
RADIUS = 6
WINDOW = 13
TL = 12
TJ = 8
CELLS = TL * TJ
HALF = 40
KEYS = 512
NEG = -1e30
MIB = 1024 * 1024


def params(mib):
    return pltpu.CompilerParams(vmem_limit_bytes=mib * MIB)


def vspec():
    return pl.BlockSpec(memory_space=pltpu.VMEM)


def anyspec():
    return pl.BlockSpec(memory_space=pl.ANY)


def sspec():
    return pl.BlockSpec(memory_space=pltpu.SMEM)


def edge_kernel(k_hbm, v_hbm, up_ref, down_ref, buf, sems):
    copies = [pltpu.make_async_copy(ref, buf.at[at], sems.at[at]) for at, ref in enumerate((k_hbm, v_hbm))]
    for copy in copies:
        copy.start()
    row = lax.broadcasted_iota(jnp.int32, (2 * HALF, CELLS), 0)
    col = lax.broadcasted_iota(jnp.int32, (2 * HALF, CELLS), 1)
    half = jnp.where(row >= HALF, 1, 0)
    r = row - half * HALF
    lon = half * 6 + r // 6
    lat = r % 6
    real = r < 36
    first = (real & (col == lon * TJ + lat)).astype(jnp.float32).astype(jnp.bfloat16)
    last = (real & (col == lon * TJ + lat + 2)).astype(jnp.float32).astype(jnp.bfloat16)
    for at, copy in enumerate(copies):
        copy.wait()
        x = buf[at]
        up_ref[at] = jnp.dot(last, x, preferred_element_type=jnp.float32).astype(jnp.bfloat16)
        down_ref[at] = jnp.dot(first, x, preferred_element_type=jnp.float32).astype(jnp.bfloat16)


def edges(k, v):
    shape = jax.ShapeDtypeStruct((2, 2 * HALF, k.shape[1]), jnp.bfloat16)
    return pl.pallas_call(
        edge_kernel,
        out_shape=(shape, shape),
        in_specs=[anyspec()] * 2,
        out_specs=(vspec(), vspec()),
        scratch_shapes=[pltpu.VMEM((2,) + k.shape, jnp.bfloat16), pltpu.SemaphoreType.DMA((2,))],
        compiler_params=params(6),
        name="edges",
    )(k, v)


def side_kernel(low_ref, high_ref, k_ref, v_ref, after_ref, east_ref, west_ref, rows):
    row = lax.broadcasted_iota(jnp.int32, (128, 256), 0)
    col = lax.broadcasted_iota(jnp.int32, (128, 256), 1)
    low = row < HALF
    own = (row >= HALF) & (row < HALF + 48)
    first = jnp.where(low, row, jnp.where(own, 80 + row - HALF, 176 + row - HALF - 48))
    last = jnp.where(own, first + 48, first + HALF)
    pick_first = jnp.where(col == first, 1.0, 0.0).astype(jnp.bfloat16)
    pick_last = jnp.where(col == last, 1.0, 0.0).astype(jnp.bfloat16)
    for at, ref in enumerate((k_ref, v_ref)):
        rows[0:80] = low_ref[at]
        rows[80:176] = ref[...]
        rows[176:256] = high_ref[at]
        x = rows[...]
        east_ref[at] = jnp.dot(pick_last, x, preferred_element_type=jnp.float32).astype(jnp.bfloat16)
        west_ref[at] = jnp.dot(pick_first, x, preferred_element_type=jnp.float32).astype(jnp.bfloat16)


def sides(low, high, k, v, after):
    shape = jax.ShapeDtypeStruct((2, 128, k.shape[1]), jnp.bfloat16)
    return pl.pallas_call(
        side_kernel,
        out_shape=(shape, shape),
        in_specs=[vspec()] * 4 + [anyspec()],
        out_specs=(vspec(), vspec()),
        scratch_shapes=[pltpu.VMEM((256, k.shape[1]), jnp.bfloat16)],
        compiler_params=params(6),
        name="sides",
    )(low, high, k, v, after)


def key_places(shape, dim):
    col = lax.broadcasted_iota(jnp.int32, shape, dim)
    lon = 6 + col // TJ
    lat = 6 + col % TJ
    side = jnp.zeros_like(col)

    def halo(base, first_lon, lat_base, which, lon, lat, side):
        r = col - base
        here = (r >= 0) & (r < HALF)
        rr = jnp.clip(r, 0, HALF - 1)
        lon = jnp.where(here, first_lon + rr // 6, lon)
        lat = jnp.where(here, lat_base + rr % 6, lat)
        side = jnp.where(here, jnp.where(rr < 36, which, 3), side)
        return lon, lat, side

    for base, first_lon, lat_base, which in (
        (96, 6, 0, 1),
        (136, 12, 0, 1),
        (176, 6, 14, 2),
        (216, 12, 14, 2),
        (256, 0, 0, 1),
        (344, 0, 14, 2),
        (384, 18, 0, 1),
        (472, 18, 14, 2),
    ):
        lon, lat, side = halo(base, first_lon, lat_base, which, lon, lat, side)
    for base, first_lon in ((296, 0), (424, 18)):
        r = col - base
        here = (r >= 0) & (r < 48)
        rr = jnp.clip(r, 0, 47)
        lon = jnp.where(here, first_lon + rr // TJ, lon)
        lat = jnp.where(here, 6 + rr % TJ, lat)
        side = jnp.where(here, 0, side)
    return lon, lat, side


def bias_kernel(place_ref, table_ref, after_ref, out_ref):
    heads = out_ref.shape[0]
    rows = heads * TJ
    table = jnp.broadcast_to(table_ref[...][:, None, :], (heads, TJ, 256)).reshape(rows, 256)
    high = table.astype(jnp.bfloat16).astype(jnp.float32)
    mid = (table - high).astype(jnp.bfloat16).astype(jnp.float32)
    low = table - high - mid
    parts = jnp.concatenate([high, mid, low], axis=0)
    lat_of_row = lax.broadcasted_iota(jnp.int32, parts.shape, 0) % TJ
    index = lax.broadcasted_iota(jnp.int32, (256, 384), 0)
    column = lax.broadcasted_iota(jnp.int32, (1, 384), 1)
    lon_gap, key_lat = column // 20, column % 20
    strip = jnp.zeros((3 * rows, 384), jnp.float32)
    for j in range(TJ):
        here = jnp.where(lat_of_row == j, parts, 0.0).astype(jnp.bfloat16)
        fits = (key_lat >= j) & (key_lat < j + WINDOW) & (lon_gap < WINDOW)
        wanted = jnp.where(fits, lon_gap * WINDOW + key_lat - j, -1)
        hot = jnp.where(index == wanted, 1.0, 0.0).astype(jnp.bfloat16)
        strip += jnp.dot(here, hot, preferred_element_type=jnp.float32)
    strip = strip.astype(jnp.bfloat16)
    strip = jnp.concatenate([strip[:rows], strip[rows : 2 * rows], strip[2 * rows :]], axis=1)

    lon, lat, side = key_places((1, KEYS), 1)
    at_south = place_ref[3] == 0
    at_north = place_ref[3] == place_ref[4] - 1
    closed = (side == 3) | ((side == 1) & at_south) | ((side == 2) & at_north)
    row = lax.broadcasted_iota(jnp.int32, (384, KEYS), 0)
    lat_gap = lat - lax.broadcasted_iota(jnp.int32, (TJ, KEYS), 0)
    near = (lat_gap >= 0) & (lat_gap < WINDOW) & jnp.logical_not(closed)
    for i in range(TL):
        gap = lon - i
        inside = (gap >= 0) & (gap < WINDOW)
        hot = jnp.where(row == jnp.where(inside, gap * 20 + lat, -1), 1.0, 0.0).astype(jnp.bfloat16)
        hot = jnp.concatenate([hot, hot, hot], axis=0)
        found = jnp.dot(strip, hot, preferred_element_type=jnp.float32)
        found = jnp.where((near & inside)[None], found.reshape(heads, TJ, KEYS), NEG)
        out_ref[:, TJ * i : TJ * i + TJ, :] = found


def bias_table(position_bias, place, after):
    heads = position_bias.shape[0]
    table = position_bias.reshape(heads, WINDOW * WINDOW)
    table = jnp.pad(table, ((0, 0), (0, 256 - WINDOW * WINDOW)))
    return pl.pallas_call(
        bias_kernel,
        out_shape=jax.ShapeDtypeStruct((heads, CELLS, KEYS), jnp.float32),
        in_specs=[sspec(), vspec(), anyspec()],
        out_specs=vspec(),
        compiler_params=params(12),
        name="bias",
    )(place, table, after)


def pair_attention(q, k, v, bias):
    n = q.shape[0]
    lane = lax.broadcasted_iota(jnp.int32, (n, 128), 1)
    zero = jnp.zeros_like(q)
    both = jnp.concatenate([jnp.where(lane < 64, q, zero), jnp.where(lane >= 64, q, zero)], axis=0)
    scores = lax.dot_general(both, k, (((1,), (1,)), ((), ())), preferred_element_type=jnp.float32)
    if bias is not None:
        scores = scores + bias
    largest = jnp.max(scores, axis=1, keepdims=True)
    weights = jnp.exp(scores - largest)
    total = jnp.sum(weights, axis=1, keepdims=True)
    out = jnp.dot(weights.astype(jnp.bfloat16), v, preferred_element_type=jnp.float32) / total
    return jnp.where(lane < 64, out[:n], out[n:]).astype(jnp.bfloat16)


def attend_kernel(
    q_ref, k_ref, v_ref, low_ref, high_ref, west_ref, east_ref, bias_ref, out_ref, kbuf, vbuf
):
    width = q_ref.shape[1]
    for buf, own, at in ((kbuf, k_ref, 0), (vbuf, v_ref, 1)):
        buf[0:96] = own[...]
        buf[96:176] = low_ref[at]
        buf[176:256] = high_ref[at]
        buf[256:384] = west_ref[at]
        buf[384:512] = east_ref[at]
    for p in range(width // 128):
        lanes = slice(128 * p, 128 * p + 128)
        q = q_ref[:, lanes] * jnp.bfloat16(0.125)
        bias = bias_ref[2 * p : 2 * p + 2].reshape(2 * CELLS, KEYS)
        out = pair_attention(q, kbuf[:, lanes], vbuf[:, lanes], bias)
        for e in range(2):
            at = turned(2 * p + e) * 64
            out_ref[:, at : at + 64] = out[:, 64 * e : 64 * e + 64]


def turned(chunk):
    return (chunk % 4) * 4 + chunk // 4


def attend(q, k, v, low, high, west, east, bias):
    width = q.shape[1]
    return pl.pallas_call(
        attend_kernel,
        out_shape=jax.ShapeDtypeStruct(q.shape, jnp.bfloat16),
        in_specs=[vspec()] * 8,
        out_specs=vspec(),
        scratch_shapes=[
            pltpu.VMEM((KEYS, width), jnp.bfloat16),
            pltpu.VMEM((KEYS, width), jnp.bfloat16),
        ],
        compiler_params=params(16),
        name="local",
    )(q, k, v, low, high, west, east, bias)


def piece_lanes(at_ref, deep):
    core, x = at_ref[0], at_ref[1]
    half = deep // 2
    far = lax.rem(x + 2, 4) * deep
    starts = (
        x * deep,
        lax.rem(x + 3 + 2 * core, 4) * deep,
        lax.rem(x + 5 - 2 * core, 4) * deep,
        far + core * half,
        far + (1 - core) * half,
    )
    return [pl.ds(pl.multiple_of(start, half), deep if n < 3 else half) for n, start in enumerate(starts)]


def project_kernel(at_ref, x_ref, tok_ref, gain_ref, p0, p1, p2, p3, p4, hid_ref, norm_ref):
    width = x_ref.shape[1]
    total = None
    for lanes, ref in zip(piece_lanes(at_ref, width // 4), (p0, p1, p2, p3, p4)):
        term = jnp.dot(x_ref[:, lanes], ref[...], preferred_element_type=jnp.float32)
        total = term if total is None else total + term
    hidden = (tok_ref[...].astype(jnp.float32) + total).astype(jnp.bfloat16)
    hid_ref[...] = hidden
    wide = hidden.astype(jnp.float32)
    inverse = lax.rsqrt(jnp.mean(wide * wide, axis=1, keepdims=True) + 1e-06)
    normed = (wide * inverse * gain_ref[...]).astype(jnp.bfloat16)
    for chunk in range(width // 64):
        at = turned(chunk) * 64
        norm_ref[:, at : at + 64] = normed[:, 64 * chunk : 64 * chunk + 64]


def project(at, x, tok, gain, pieces):
    shape = jax.ShapeDtypeStruct(x.shape, jnp.bfloat16)
    return pl.pallas_call(
        project_kernel,
        out_shape=(shape, shape),
        in_specs=[sspec()] + [vspec()] * (3 + len(pieces)),
        out_specs=(vspec(), vspec()),
        compiler_params=params(8),
        name="project",
    )(at, x, tok, gain, *pieces)


def global_kernel(at_ref, x0, x1, x2, x3, x4, *rest):
    weights, (out_ref, xbuf) = rest[:15], rest[15:]
    width = x0.shape[1]

    @pl.when(pl.program_id(0) == 0)
    def _():
        for at, ref in enumerate((x0, x1, x2, x3, x4)):
            xbuf[CELLS * at : CELLS * at + CELLS] = ref[...]

    spans = piece_lanes(at_ref, width // 4)

    def part(rows, refs):
        total = None
        for lanes, ref in zip(spans, refs):
            term = jnp.dot(xbuf[0:rows, lanes], ref[...], preferred_element_type=jnp.float32)
            total = term if total is None else total + term
        return total.astype(jnp.bfloat16)

    q = part(CELLS, weights[0:5]) * jnp.bfloat16(0.125)
    k = part(5 * CELLS, weights[5:10])
    v = part(5 * CELLS, weights[10:15])
    for p in range(q.shape[1] // 128):
        lanes = slice(128 * p, 128 * p + 128)
        out_ref[:, lanes] = pair_attention(q[:, lanes], k[:, lanes], v[:, lanes], None)


def global_layer(at, blocks, pieces):
    cells, width = blocks[0].shape
    steps = width // 256
    whole = pl.BlockSpec((cells, width), lambda g, c: (0, 0))
    weights = [
        pl.BlockSpec((piece.shape[0], 256), lambda g, c, t=t: (0, steps * t + g)) for t in range(3) for piece in pieces
    ]
    return pl.pallas_call(
        global_kernel,
        out_shape=jax.ShapeDtypeStruct((cells, width), jnp.bfloat16),
        grid_spec=pltpu.PrefetchScalarGridSpec(
            num_scalar_prefetch=1,
            grid=(steps,),
            in_specs=[whole] * 5 + weights,
            out_specs=pl.BlockSpec((cells, 256), lambda g, c: (0, g)),
            scratch_shapes=[pltpu.VMEM((5 * cells, width), jnp.bfloat16)],
        ),
        compiler_params=params(20),
        name="global",
    )(at, *blocks, *(pieces * 3))


def place_kernel(at_ref, p0, p1, p2, p3, p4, *rest):
    out_ref = rest[-1]
    rows = p0.shape[0]
    half = rows // 2
    core, zh = at_ref[0], at_ref[2]
    far = lax.rem(zh + 2, 4) * rows
    starts = (
        zh * rows,
        lax.rem(zh + 3 + 2 * core, 4) * rows,
        lax.rem(zh + 5 - 2 * core, 4) * rows,
        far + core * half,
        far + (1 - core) * half,
    )
    for start, ref in zip(starts, (p0, p1, p2, p3, p4)):
        to = pl.ds(pl.multiple_of(start, half), ref.shape[0])
        out_ref[to] = ref[...]


def place_rows(at, pieces, after):
    rows, columns = pieces[0].shape
    return pl.pallas_call(
        place_kernel,
        out_shape=jax.ShapeDtypeStruct((rows * 4, columns), pieces[0].dtype),
        in_specs=[sspec()] + [vspec()] * len(pieces) + [anyspec()] * len(after),
        out_specs=vspec(),
        compiler_params=params(8),
        name="place",
    )(at, *pieces, *after)


def half_kernel(at_ref, x_ref, *rest):
    out_ref = rest[-1]
    rows = out_ref.shape[0]
    out_ref[...] = x_ref[pl.ds(pl.multiple_of(at_ref[0] * rows, rows), rows)]


def half_of(at, x, after):
    return pl.pallas_call(
        half_kernel,
        out_shape=jax.ShapeDtypeStruct((x.shape[0] // 2, x.shape[1]), x.dtype),
        in_specs=[sspec(), vspec()] + [anyspec()] * len(after),
        out_specs=vspec(),
        compiler_params=params(8),
        name="half",
    )(at, x, *after)


def gathered(rows, axis, at, after):
    roles = [(i, (i + 1) % 4) for i in range(4)] + [(4 + i, 4 + (i + 3) % 4) for i in range(4)]
    swap = [(0, 1), (1, 0)]
    near = lax.ppermute(rows, ("c", axis), roles)
    far = lax.ppermute(half_of(at, near, after), ("c", axis), roles)
    return [rows, near, lax.ppermute(near, "c", swap), far, lax.ppermute(far, "c", swap)]


def ring(count, by):
    return [(i, (i + by) % count) for i in range(count)]


def body(tokens, query_local, key_local, value_local, position_bias, output_weight, norm_gain, global_weight):
    width = tokens.shape[2]
    flat = lambda a: a.reshape(CELLS, width)
    q, k, v, tok = flat(query_local), flat(key_local), flat(value_local), flat(tokens)
    core = lax.axis_index("c")
    lat = lax.axis_index(LAT)
    lat_count = lax.axis_size(LAT)
    lon_count = lax.axis_size(LON)
    xs, zs = lax.axis_size("x"), lax.axis_size("zh")
    x, zh = lax.axis_index("x"), lax.axis_index("zh")
    at = jnp.stack([core, x, zh, lat, jnp.int32(lat_count)]).astype(jnp.int32)
    up, down = edges(k, v)
    low = lax.ppermute(up, LAT, [(i, i + 1) for i in range(lat_count - 1)])
    high = lax.ppermute(down, LAT, [(i + 1, i) for i in range(lat_count - 1)])
    bias = bias_table(position_bias, at, up)
    pieces_o = gathered(output_weight, "zh", at, [up])
    to_east, to_west = sides(low, high, k, v, bias)
    west = lax.ppermute(to_east, LON, ring(lon_count, 1))
    east = lax.ppermute(to_west, LON, ring(lon_count, -1))
    rows_o = place_rows(at, pieces_o, [to_east, to_west])
    global_weight, pieces_o[3] = lax.optimization_barrier((global_weight, pieces_o[3]))
    pieces_g = gathered(global_weight, "zh", at, [rows_o])
    pieces_o = gathered(rows_o, "x", at, [west, east])
    local_out = attend(q, k, v, low, high, west, east, bias)
    rows_g = place_rows(at, pieces_g, [pieces_o[3], local_out])
    hidden, normed = project(at, local_out, tok, norm_gain.reshape(1, width), pieces_o)
    behind = lax.ppermute(normed, LON + ("zh",), ring(lon_count * zs, 1))
    blocks = [normed]
    for by in range(1, xs):
        sent = jnp.where(x + by < xs, normed, behind)
        blocks.append(lax.ppermute(sent, "x", ring(xs, by)))
    blocks.append(behind)
    pieces_g = gathered(rows_g, "x", at, blocks[1:xs])
    attended = global_layer(at, blocks, pieces_g)
    return hidden.reshape(tokens.shape), attended.reshape(tokens.shape)


def solution(mesh):
    fine = Mesh(mesh.devices.reshape(2, 8, 2, 4, 4), LON + LAT)
    grid = P(LON, LAT, None)
    return jax.shard_map(
        body,
        mesh=fine,
        in_specs=(grid, grid, grid, grid, P(), P(LAT, None), P(), P(LAT, None)),
        out_specs=(grid, grid),
        check_vma=False,
    )
```

```python
import functools
import math

import jax
import jax.numpy as jnp
from jax import lax
from jax.experimental import pallas as pl
from jax.experimental.pallas import tpu as pltpu
from jax.sharding import Mesh, PartitionSpec as P

LON = ("zl", "y", "c")
LAT = ("zh", "x")
RADIUS = 6
WINDOW = 13
TL = 12
TJ = 8
CELLS = TL * TJ
HALF = 40
KEYS = 512
NEG = -1e30
MIB = 1024 * 1024


def params(mib):
    return pltpu.CompilerParams(vmem_limit_bytes=mib * MIB)


def vspec():
    return pl.BlockSpec(memory_space=pltpu.VMEM)


def anyspec():
    return pl.BlockSpec(memory_space=pl.ANY)


def sspec():
    return pl.BlockSpec(memory_space=pltpu.SMEM)


def edge_kernel(k_hbm, v_hbm, up_ref, down_ref, buf, sems):
    copies = [pltpu.make_async_copy(ref, buf.at[at], sems.at[at]) for at, ref in enumerate((k_hbm, v_hbm))]
    for copy in copies:
        copy.start()
    row = lax.broadcasted_iota(jnp.int32, (2 * HALF, CELLS), 0)
    col = lax.broadcasted_iota(jnp.int32, (2 * HALF, CELLS), 1)
    half = jnp.where(row >= HALF, 1, 0)
    r = row - half * HALF
    lon = half * 6 + r // 6
    lat = r % 6
    real = r < 36
    first = (real & (col == lon * TJ + lat)).astype(jnp.float32).astype(jnp.bfloat16)
    last = (real & (col == lon * TJ + lat + 2)).astype(jnp.float32).astype(jnp.bfloat16)
    for at, copy in enumerate(copies):
        copy.wait()
        x = buf[at]
        up_ref[at] = jnp.dot(last, x, preferred_element_type=jnp.float32).astype(jnp.bfloat16)
        down_ref[at] = jnp.dot(first, x, preferred_element_type=jnp.float32).astype(jnp.bfloat16)


def edges(k, v):
    shape = jax.ShapeDtypeStruct((2, 2 * HALF, k.shape[1]), jnp.bfloat16)
    return pl.pallas_call(
        edge_kernel,
        out_shape=(shape, shape),
        in_specs=[anyspec()] * 2,
        out_specs=(vspec(), vspec()),
        scratch_shapes=[pltpu.VMEM((2,) + k.shape, jnp.bfloat16), pltpu.SemaphoreType.DMA((2,))],
        compiler_params=params(6),
        name="edges",
    )(k, v)


def side_kernel(low_ref, high_ref, k_ref, v_ref, after_ref, east_ref, west_ref, rows):
    row = lax.broadcasted_iota(jnp.int32, (128, 256), 0)
    col = lax.broadcasted_iota(jnp.int32, (128, 256), 1)
    low = row < HALF
    own = (row >= HALF) & (row < HALF + 48)
    first = jnp.where(low, row, jnp.where(own, 80 + row - HALF, 176 + row - HALF - 48))
    last = jnp.where(own, first + 48, first + HALF)
    pick_first = jnp.where(col == first, 1.0, 0.0).astype(jnp.bfloat16)
    pick_last = jnp.where(col == last, 1.0, 0.0).astype(jnp.bfloat16)
    for at, ref in enumerate((k_ref, v_ref)):
        rows[0:80] = low_ref[at]
        rows[80:176] = ref[...]
        rows[176:256] = high_ref[at]
        x = rows[...]
        east_ref[at] = jnp.dot(pick_last, x, preferred_element_type=jnp.float32).astype(jnp.bfloat16)
        west_ref[at] = jnp.dot(pick_first, x, preferred_element_type=jnp.float32).astype(jnp.bfloat16)


def sides(low, high, k, v, after):
    shape = jax.ShapeDtypeStruct((2, 128, k.shape[1]), jnp.bfloat16)
    return pl.pallas_call(
        side_kernel,
        out_shape=(shape, shape),
        in_specs=[vspec()] * 4 + [anyspec()],
        out_specs=(vspec(), vspec()),
        scratch_shapes=[pltpu.VMEM((256, k.shape[1]), jnp.bfloat16)],
        compiler_params=params(6),
        name="sides",
    )(low, high, k, v, after)


def key_places(shape, dim):
    col = lax.broadcasted_iota(jnp.int32, shape, dim)
    lon = 6 + col // TJ
    lat = 6 + col % TJ
    side = jnp.zeros_like(col)

    def halo(base, first_lon, lat_base, which, lon, lat, side):
        r = col - base
        here = (r >= 0) & (r < HALF)
        rr = jnp.clip(r, 0, HALF - 1)
        lon = jnp.where(here, first_lon + rr // 6, lon)
        lat = jnp.where(here, lat_base + rr % 6, lat)
        side = jnp.where(here, jnp.where(rr < 36, which, 3), side)
        return lon, lat, side

    for base, first_lon, lat_base, which in (
        (96, 6, 0, 1),
        (136, 12, 0, 1),
        (176, 6, 14, 2),
        (216, 12, 14, 2),
        (256, 0, 0, 1),
        (344, 0, 14, 2),
        (384, 18, 0, 1),
        (472, 18, 14, 2),
    ):
        lon, lat, side = halo(base, first_lon, lat_base, which, lon, lat, side)
    for base, first_lon in ((296, 0), (424, 18)):
        r = col - base
        here = (r >= 0) & (r < 48)
        rr = jnp.clip(r, 0, 47)
        lon = jnp.where(here, first_lon + rr // TJ, lon)
        lat = jnp.where(here, 6 + rr % TJ, lat)
        side = jnp.where(here, 0, side)
    return lon, lat, side


def bias_kernel(place_ref, table_ref, after_ref, out_ref):
    heads = out_ref.shape[0]
    rows = heads * TJ
    table = jnp.broadcast_to(table_ref[...][:, None, :], (heads, TJ, 256)).reshape(rows, 256)
    high = table.astype(jnp.bfloat16).astype(jnp.float32)
    mid = (table - high).astype(jnp.bfloat16).astype(jnp.float32)
    low = table - high - mid
    parts = jnp.concatenate([high, mid, low], axis=0)
    lat_of_row = lax.broadcasted_iota(jnp.int32, parts.shape, 0) % TJ
    index = lax.broadcasted_iota(jnp.int32, (256, 384), 0)
    column = lax.broadcasted_iota(jnp.int32, (1, 384), 1)
    lon_gap, key_lat = column // 20, column % 20
    strip = jnp.zeros((3 * rows, 384), jnp.float32)
    for j in range(TJ):
        here = jnp.where(lat_of_row == j, parts, 0.0).astype(jnp.bfloat16)
        fits = (key_lat >= j) & (key_lat < j + WINDOW) & (lon_gap < WINDOW)
        wanted = jnp.where(fits, lon_gap * WINDOW + key_lat - j, -1)
        hot = jnp.where(index == wanted, 1.0, 0.0).astype(jnp.bfloat16)
        strip += jnp.dot(here, hot, preferred_element_type=jnp.float32)
    strip = strip.astype(jnp.bfloat16)
    strip = jnp.concatenate([strip[:rows], strip[rows : 2 * rows], strip[2 * rows :]], axis=1)

    lon, lat, side = key_places((1, KEYS), 1)
    at_south = place_ref[3] == 0
    at_north = place_ref[3] == place_ref[4] - 1
    closed = (side == 3) | ((side == 1) & at_south) | ((side == 2) & at_north)
    row = lax.broadcasted_iota(jnp.int32, (384, KEYS), 0)
    lat_gap = lat - lax.broadcasted_iota(jnp.int32, (TJ, KEYS), 0)
    near = (lat_gap >= 0) & (lat_gap < WINDOW) & jnp.logical_not(closed)
    for i in range(TL):
        gap = lon - i
        inside = (gap >= 0) & (gap < WINDOW)
        hot = jnp.where(row == jnp.where(inside, gap * 20 + lat, -1), 1.0, 0.0).astype(jnp.bfloat16)
        hot = jnp.concatenate([hot, hot, hot], axis=0)
        found = jnp.dot(strip, hot, preferred_element_type=jnp.float32)
        found = jnp.where((near & inside)[None], found.reshape(heads, TJ, KEYS), NEG)
        out_ref[:, TJ * i : TJ * i + TJ, :] = found


def bias_table(position_bias, place, after):
    heads = position_bias.shape[0]
    table = position_bias.reshape(heads, WINDOW * WINDOW)
    table = jnp.pad(table, ((0, 0), (0, 256 - WINDOW * WINDOW)))
    return pl.pallas_call(
        bias_kernel,
        out_shape=jax.ShapeDtypeStruct((heads, CELLS, KEYS), jnp.float32),
        in_specs=[sspec(), vspec(), anyspec()],
        out_specs=vspec(),
        compiler_params=params(12),
        name="bias",
    )(place, table, after)


def pair_attention(q, k, v, bias):
    n = q.shape[0]
    lane = lax.broadcasted_iota(jnp.int32, (n, 128), 1)
    zero = jnp.zeros_like(q)
    both = jnp.concatenate([jnp.where(lane < 64, q, zero), jnp.where(lane >= 64, q, zero)], axis=0)
    scores = lax.dot_general(both, k, (((1,), (1,)), ((), ())), preferred_element_type=jnp.float32)
    if bias is not None:
        scores = scores + bias
    largest = jnp.max(scores, axis=1, keepdims=True)
    weights = jnp.exp(scores - largest)
    total = jnp.sum(weights, axis=1, keepdims=True)
    out = jnp.dot(weights.astype(jnp.bfloat16), v, preferred_element_type=jnp.float32) / total
    return jnp.where(lane < 64, out[:n], out[n:]).astype(jnp.bfloat16)


def attend_kernel(
    q_ref, k_ref, v_ref, low_ref, high_ref, west_ref, east_ref, bias_ref, out_ref, kbuf, vbuf
):
    width = q_ref.shape[1]
    for buf, own, at in ((kbuf, k_ref, 0), (vbuf, v_ref, 1)):
        buf[0:96] = own[...]
        buf[96:176] = low_ref[at]
        buf[176:256] = high_ref[at]
        buf[256:384] = west_ref[at]
        buf[384:512] = east_ref[at]
    for p in range(width // 128):
        lanes = slice(128 * p, 128 * p + 128)
        q = q_ref[:, lanes] * jnp.bfloat16(0.125)
        bias = bias_ref[2 * p : 2 * p + 2].reshape(2 * CELLS, KEYS)
        out = pair_attention(q, kbuf[:, lanes], vbuf[:, lanes], bias)
        for e in range(2):
            at = turned(2 * p + e) * 64
            out_ref[:, at : at + 64] = out[:, 64 * e : 64 * e + 64]


def turned(chunk):
    return (chunk % 4) * 4 + chunk // 4


def attend(q, k, v, low, high, west, east, bias):
    width = q.shape[1]
    return pl.pallas_call(
        attend_kernel,
        out_shape=jax.ShapeDtypeStruct(q.shape, jnp.bfloat16),
        in_specs=[vspec()] * 8,
        out_specs=vspec(),
        scratch_shapes=[
            pltpu.VMEM((KEYS, width), jnp.bfloat16),
            pltpu.VMEM((KEYS, width), jnp.bfloat16),
        ],
        compiler_params=params(16),
        name="local",
    )(q, k, v, low, high, west, east, bias)


def piece_lanes(at_ref, deep):
    core, x = at_ref[0], at_ref[1]
    half = deep // 2
    far = lax.rem(x + 2, 4) * deep
    starts = (
        x * deep,
        lax.rem(x + 3 + 2 * core, 4) * deep,
        lax.rem(x + 5 - 2 * core, 4) * deep,
        far + core * half,
        far + (1 - core) * half,
    )
    return [pl.ds(pl.multiple_of(start, half), deep if n < 3 else half) for n, start in enumerate(starts)]


def project_kernel(at_ref, x_ref, tok_ref, gain_ref, p0, p1, p2, p3, hid_ref, norm_ref):
    width = x_ref.shape[1]
    total = None
    for lanes, ref in zip(piece_lanes(at_ref, width // 4), unpacked(p0, p1, p2, p3)):
        term = jnp.dot(x_ref[:, lanes], ref[...], preferred_element_type=jnp.float32)
        total = term if total is None else total + term
    hidden = (tok_ref[...].astype(jnp.float32) + total).astype(jnp.bfloat16)
    hid_ref[...] = hidden
    wide = hidden.astype(jnp.float32)
    inverse = lax.rsqrt(jnp.mean(wide * wide, axis=1, keepdims=True) + 1e-06)
    normed = (wide * inverse * gain_ref[...]).astype(jnp.bfloat16)
    for chunk in range(width // 64):
        at = turned(chunk) * 64
        norm_ref[:, at : at + 64] = normed[:, 64 * chunk : 64 * chunk + 64]


def project(at, x, tok, gain, pieces):
    shape = jax.ShapeDtypeStruct(x.shape, jnp.bfloat16)
    return pl.pallas_call(
        project_kernel,
        out_shape=(shape, shape),
        in_specs=[sspec()] + [vspec()] * (3 + len(pieces)),
        out_specs=(vspec(), vspec()),
        compiler_params=params(8),
        name="project",
    )(at, x, tok, gain, *pieces)


def global_kernel(at_ref, own_ref, slots_ref, *rest):
    weights, (out_ref, xbuf) = rest[:15], rest[15:]
    width = own_ref.shape[1]

    @pl.when(pl.program_id(0) == 0)
    def _():
        xbuf[0:CELLS] = own_ref[...]
        for at in range(4):
            xbuf[CELLS * at + CELLS : CELLS * at + 2 * CELLS] = slots_ref[at]

    spans = piece_lanes(at_ref, width // 4)

    def part(rows, refs):
        total = None
        for lanes, ref in zip(spans, refs):
            term = jnp.dot(xbuf[0:rows, lanes], ref[...], preferred_element_type=jnp.float32)
            total = term if total is None else total + term
        return total.astype(jnp.bfloat16)

    q = part(CELLS, weights[0:5]) * jnp.bfloat16(0.125)
    k = part(5 * CELLS, weights[5:10])
    v = part(5 * CELLS, weights[10:15])
    for p in range(q.shape[1] // 128):
        lanes = slice(128 * p, 128 * p + 128)
        out_ref[:, lanes] = pair_attention(q[:, lanes], k[:, lanes], v[:, lanes], None)


def global_layer(at, own, slots, pieces):
    cells, width = own.shape
    steps = width // 256
    whole = [
        pl.BlockSpec((cells, width), lambda g, c: (0, 0)),
        pl.BlockSpec(slots.shape, lambda g, c: (0, 0, 0)),
    ]
    weights = [
        pl.BlockSpec((piece.shape[0], 256), lambda g, c, t=t: (0, steps * t + g)) for t in range(3) for piece in pieces
    ]
    return pl.pallas_call(
        global_kernel,
        out_shape=jax.ShapeDtypeStruct((cells, width), jnp.bfloat16),
        grid_spec=pltpu.PrefetchScalarGridSpec(
            num_scalar_prefetch=1,
            grid=(steps,),
            in_specs=whole + weights,
            out_specs=pl.BlockSpec((cells, 256), lambda g, c: (0, g)),
            scratch_shapes=[pltpu.VMEM((5 * cells, width), jnp.bfloat16)],
        ),
        compiler_params=params(20),
        name="global",
    )(at, own, slots, *(pieces * 3))


def place_kernel(at_ref, p0, p1, p2, p3, *rest):
    out_ref = rest[-1]
    rows = p0.shape[0]
    half = rows // 2
    core, zh = at_ref[0], at_ref[2]
    far = lax.rem(zh + 2, 4) * rows
    starts = (
        zh * rows,
        lax.rem(zh + 3 + 2 * core, 4) * rows,
        lax.rem(zh + 5 - 2 * core, 4) * rows,
        far + core * half,
        far + (1 - core) * half,
    )
    for start, ref in zip(starts, unpacked(p0, p1, p2, p3)):
        to = pl.ds(pl.multiple_of(start, half), ref.shape[0])
        out_ref[to] = ref[...]


def place_rows(at, pieces, after):
    rows, columns = pieces[0].shape
    return pl.pallas_call(
        place_kernel,
        out_shape=jax.ShapeDtypeStruct((rows * 4, columns), pieces[0].dtype),
        in_specs=[sspec()] + [vspec()] * len(pieces) + [anyspec()] * len(after),
        out_specs=vspec(),
        compiler_params=params(8),
        name="place",
    )(at, *pieces, *after)


def half_kernel(at_ref, x_ref, *rest):
    out_ref = rest[-1]
    rows = out_ref.shape[0]
    out_ref[...] = x_ref[pl.ds(pl.multiple_of(at_ref[0] * rows, rows), rows)]


def half_of(at, x, after):
    return pl.pallas_call(
        half_kernel,
        out_shape=jax.ShapeDtypeStruct((x.shape[0] // 2, x.shape[1]), x.dtype),
        in_specs=[sspec(), vspec()] + [anyspec()] * len(after),
        out_specs=vspec(),
        compiler_params=params(8),
        name="half",
    )(at, x, *after)


def pack_kernel(a_ref, b_ref, out_ref):
    rows = a_ref.shape[0]
    out_ref[0:rows] = a_ref[...]
    out_ref[rows : rows + b_ref.shape[0]] = b_ref[...]


def pack(a, b):
    return pl.pallas_call(
        pack_kernel,
        out_shape=jax.ShapeDtypeStruct((a.shape[0] + b.shape[0], a.shape[1]), a.dtype),
        in_specs=[vspec(), vspec()],
        out_specs=vspec(),
        compiler_params=params(8),
        name="pack",
    )(a, b)


SWAP = [(0, 1), (1, 0)]
ROLES = [(i, (i + 1) % 4) for i in range(4)] + [(4 + i, 4 + (i + 3) % 4) for i in range(4)]


def gathered(rows, axis, at, after):
    near = lax.ppermute(rows, ("c", axis), ROLES)
    far = lax.ppermute(half_of(at, near, after), ("c", axis), ROLES)
    return [rows, near, far, lax.ppermute(pack(near, far), "c", SWAP)]


def unpacked(own, near, far, others):
    rows = own.shape[0]
    return [own, near, others.at[0:rows], far, others.at[rows : rows + rows // 2]]


def spread_kernel(at_ref, own_ref, behind_ref, after_ref, out_ref):
    for slot in range(4):
        out_ref[slot] = jnp.where(slot > at_ref[1], own_ref[...], behind_ref[...])


def spread(at, own, behind, after):
    return pl.pallas_call(
        spread_kernel,
        out_shape=jax.ShapeDtypeStruct((4,) + own.shape, own.dtype),
        in_specs=[sspec(), vspec(), vspec(), anyspec()],
        out_specs=vspec(),
        compiler_params=params(8),
        name="spread",
    )(at, own, behind, after)


def ring(count, by):
    return [(i, (i + by) % count) for i in range(count)]


def body(tokens, query_local, key_local, value_local, position_bias, output_weight, norm_gain, global_weight):
    width = tokens.shape[2]
    flat = lambda a: a.reshape(CELLS, width)
    q, k, v, tok = flat(query_local), flat(key_local), flat(value_local), flat(tokens)
    core = lax.axis_index("c")
    lat = lax.axis_index(LAT)
    lat_count = lax.axis_size(LAT)
    lon_count = lax.axis_size(LON)
    xs, zs = lax.axis_size("x"), lax.axis_size("zh")
    x, zh = lax.axis_index("x"), lax.axis_index("zh")
    at = jnp.stack([core, x, zh, lat, jnp.int32(lat_count)]).astype(jnp.int32)
    up, down = edges(k, v)
    low = lax.ppermute(up, LAT, [(i, i + 1) for i in range(lat_count - 1)])
    high = lax.ppermute(down, LAT, [(i + 1, i) for i in range(lat_count - 1)])
    bias = bias_table(position_bias, at, up)
    pieces_o = gathered(output_weight, "zh", at, [bias])
    to_east, to_west = sides(low, high, k, v, bias)
    west = lax.ppermute(to_east, LON, ring(lon_count, 1))
    east = lax.ppermute(to_west, LON, ring(lon_count, -1))
    rows_o = place_rows(at, pieces_o, [to_east, to_west])
    global_weight, to_east, pieces_o[2] = lax.optimization_barrier((global_weight, to_east, pieces_o[2]))
    pieces_g = gathered(global_weight, "zh", at, [rows_o])
    pieces_o = gathered(rows_o, "x", at, [west, east])
    local_out = attend(q, k, v, low, high, west, east, bias)
    rows_g = place_rows(at, pieces_g, [pieces_o[2], local_out])
    hidden, normed = project(at, local_out, tok, norm_gain.reshape(1, width), pieces_o)
    behind = lax.ppermute(normed, LON + ("zh",), ring(lon_count * zs, 1))
    near = lax.ppermute(rows_g, ("c", "x"), ROLES)
    half = half_of(at, near, [behind])
    far = lax.ppermute(half, ("c", "x"), ROLES)
    slots = lax.all_to_all(spread(at, normed, behind, half), "x", 0, 0)
    near_other = lax.ppermute(near, "c", SWAP)
    late, slots = lax.optimization_barrier((far, slots))
    far_other = lax.ppermute(late, "c", SWAP)
    attended = global_layer(at, normed, slots, [rows_g, near, near_other, late, far_other])
    return hidden.reshape(tokens.shape), attended.reshape(tokens.shape)


def solution(mesh):
    fine = Mesh(mesh.devices.reshape(2, 8, 2, 4, 4), LON + LAT)
    grid = P(LON, LAT, None)
    return jax.shard_map(
        body,
        mesh=fine,
        in_specs=(grid, grid, grid, grid, P(), P(LAT, None), P(), P(LAT, None)),
        out_specs=(grid, grid),
        check_vma=False,
    )
```

```python
import functools
import math

import jax
import jax.numpy as jnp
from jax import lax
from jax.experimental import pallas as pl
from jax.experimental.pallas import tpu as pltpu
from jax.sharding import Mesh, PartitionSpec as P

LON = ("zl", "y", "c")
LAT = ("zh", "x")
RADIUS = 6
WINDOW = 13
TL = 12
TJ = 8
CELLS = TL * TJ
HALF = 40
KEYS = 512
NEG = -1e30
MIB = 1024 * 1024


def params(mib):
    return pltpu.CompilerParams(vmem_limit_bytes=mib * MIB)


def vspec():
    return pl.BlockSpec(memory_space=pltpu.VMEM)


def anyspec():
    return pl.BlockSpec(memory_space=pl.ANY)


def sspec():
    return pl.BlockSpec(memory_space=pltpu.SMEM)


def edge_kernel(k_hbm, v_hbm, up_ref, down_ref, buf, sems):
    copies = [pltpu.make_async_copy(ref, buf.at[at], sems.at[at]) for at, ref in enumerate((k_hbm, v_hbm))]
    for copy in copies:
        copy.start()
    row = lax.broadcasted_iota(jnp.int32, (2 * HALF, CELLS), 0)
    col = lax.broadcasted_iota(jnp.int32, (2 * HALF, CELLS), 1)
    half = jnp.where(row >= HALF, 1, 0)
    r = row - half * HALF
    lon = half * 6 + r // 6
    lat = r % 6
    real = r < 36
    first = (real & (col == lon * TJ + lat)).astype(jnp.float32).astype(jnp.bfloat16)
    last = (real & (col == lon * TJ + lat + 2)).astype(jnp.float32).astype(jnp.bfloat16)
    for at, copy in enumerate(copies):
        copy.wait()
        x = buf[at]
        up_ref[at] = jnp.dot(last, x, preferred_element_type=jnp.float32).astype(jnp.bfloat16)
        down_ref[at] = jnp.dot(first, x, preferred_element_type=jnp.float32).astype(jnp.bfloat16)


def edges(k, v):
    shape = jax.ShapeDtypeStruct((2, 2 * HALF, k.shape[1]), jnp.bfloat16)
    return pl.pallas_call(
        edge_kernel,
        out_shape=(shape, shape),
        in_specs=[anyspec()] * 2,
        out_specs=(vspec(), vspec()),
        scratch_shapes=[pltpu.VMEM((2,) + k.shape, jnp.bfloat16), pltpu.SemaphoreType.DMA((2,))],
        compiler_params=params(6),
        name="edges",
    )(k, v)


def side_kernel(low_ref, high_ref, k_ref, v_ref, after_ref, east_ref, west_ref, rows):
    row = lax.broadcasted_iota(jnp.int32, (128, 256), 0)
    col = lax.broadcasted_iota(jnp.int32, (128, 256), 1)
    low = row < HALF
    own = (row >= HALF) & (row < HALF + 48)
    first = jnp.where(low, row, jnp.where(own, 80 + row - HALF, 176 + row - HALF - 48))
    last = jnp.where(own, first + 48, first + HALF)
    pick_first = jnp.where(col == first, 1.0, 0.0).astype(jnp.bfloat16)
    pick_last = jnp.where(col == last, 1.0, 0.0).astype(jnp.bfloat16)
    for at, ref in enumerate((k_ref, v_ref)):
        rows[0:80] = low_ref[at]
        rows[80:176] = ref[...]
        rows[176:256] = high_ref[at]
        x = rows[...]
        east_ref[at] = jnp.dot(pick_last, x, preferred_element_type=jnp.float32).astype(jnp.bfloat16)
        west_ref[at] = jnp.dot(pick_first, x, preferred_element_type=jnp.float32).astype(jnp.bfloat16)


def sides(low, high, k, v, after):
    shape = jax.ShapeDtypeStruct((2, 128, k.shape[1]), jnp.bfloat16)
    return pl.pallas_call(
        side_kernel,
        out_shape=(shape, shape),
        in_specs=[vspec()] * 4 + [anyspec()],
        out_specs=(vspec(), vspec()),
        scratch_shapes=[pltpu.VMEM((256, k.shape[1]), jnp.bfloat16)],
        compiler_params=params(6),
        name="sides",
    )(low, high, k, v, after)


def key_places(shape, dim):
    col = lax.broadcasted_iota(jnp.int32, shape, dim)
    lon = 6 + col // TJ
    lat = 6 + col % TJ
    side = jnp.zeros_like(col)

    def halo(base, first_lon, lat_base, which, lon, lat, side):
        r = col - base
        here = (r >= 0) & (r < HALF)
        rr = jnp.clip(r, 0, HALF - 1)
        lon = jnp.where(here, first_lon + rr // 6, lon)
        lat = jnp.where(here, lat_base + rr % 6, lat)
        side = jnp.where(here, jnp.where(rr < 36, which, 3), side)
        return lon, lat, side

    for base, first_lon, lat_base, which in (
        (96, 6, 0, 1),
        (136, 12, 0, 1),
        (176, 6, 14, 2),
        (216, 12, 14, 2),
        (256, 0, 0, 1),
        (344, 0, 14, 2),
        (384, 18, 0, 1),
        (472, 18, 14, 2),
    ):
        lon, lat, side = halo(base, first_lon, lat_base, which, lon, lat, side)
    for base, first_lon in ((296, 0), (424, 18)):
        r = col - base
        here = (r >= 0) & (r < 48)
        rr = jnp.clip(r, 0, 47)
        lon = jnp.where(here, first_lon + rr // TJ, lon)
        lat = jnp.where(here, 6 + rr % TJ, lat)
        side = jnp.where(here, 0, side)
    return lon, lat, side


def bias_kernel(place_ref, table_ref, after_ref, out_ref):
    heads = out_ref.shape[0]
    rows = heads * TJ
    table = jnp.broadcast_to(table_ref[...][:, None, :], (heads, TJ, 256)).reshape(rows, 256)
    high = table.astype(jnp.bfloat16).astype(jnp.float32)
    mid = (table - high).astype(jnp.bfloat16).astype(jnp.float32)
    low = table - high - mid
    parts = jnp.concatenate([high, mid, low], axis=0)
    lat_of_row = lax.broadcasted_iota(jnp.int32, parts.shape, 0) % TJ
    index = lax.broadcasted_iota(jnp.int32, (256, 384), 0)
    column = lax.broadcasted_iota(jnp.int32, (1, 384), 1)
    lon_gap, key_lat = column // 20, column % 20
    strip = jnp.zeros((3 * rows, 384), jnp.float32)
    for j in range(TJ):
        here = jnp.where(lat_of_row == j, parts, 0.0).astype(jnp.bfloat16)
        fits = (key_lat >= j) & (key_lat < j + WINDOW) & (lon_gap < WINDOW)
        wanted = jnp.where(fits, lon_gap * WINDOW + key_lat - j, -1)
        hot = jnp.where(index == wanted, 1.0, 0.0).astype(jnp.bfloat16)
        strip += jnp.dot(here, hot, preferred_element_type=jnp.float32)
    strip = strip.astype(jnp.bfloat16)
    strip = jnp.concatenate([strip[:rows], strip[rows : 2 * rows], strip[2 * rows :]], axis=1)

    lon, lat, side = key_places((1, KEYS), 1)
    at_south = place_ref[3] == 0
    at_north = place_ref[3] == place_ref[4] - 1
    closed = (side == 3) | ((side == 1) & at_south) | ((side == 2) & at_north)
    row = lax.broadcasted_iota(jnp.int32, (384, KEYS), 0)
    lat_gap = lat - lax.broadcasted_iota(jnp.int32, (TJ, KEYS), 0)
    near = (lat_gap >= 0) & (lat_gap < WINDOW) & jnp.logical_not(closed)
    for i in range(TL):
        gap = lon - i
        inside = (gap >= 0) & (gap < WINDOW)
        hot = jnp.where(row == jnp.where(inside, gap * 20 + lat, -1), 1.0, 0.0).astype(jnp.bfloat16)
        hot = jnp.concatenate([hot, hot, hot], axis=0)
        found = jnp.dot(strip, hot, preferred_element_type=jnp.float32)
        found = jnp.where((near & inside)[None], found.reshape(heads, TJ, KEYS), NEG)
        out_ref[:, TJ * i : TJ * i + TJ, :] = found


def bias_table(position_bias, place, after):
    heads = position_bias.shape[0]
    table = position_bias.reshape(heads, WINDOW * WINDOW)
    table = jnp.pad(table, ((0, 0), (0, 256 - WINDOW * WINDOW)))
    return pl.pallas_call(
        bias_kernel,
        out_shape=jax.ShapeDtypeStruct((heads, CELLS, KEYS), jnp.float32),
        in_specs=[sspec(), vspec(), anyspec()],
        out_specs=vspec(),
        compiler_params=params(12),
        name="bias",
    )(place, table, after)


def pair_attention(q, k, v, bias):
    n = q.shape[0]
    lane = lax.broadcasted_iota(jnp.int32, (n, 128), 1)
    zero = jnp.zeros_like(q)
    both = jnp.concatenate([jnp.where(lane < 64, q, zero), jnp.where(lane >= 64, q, zero)], axis=0)
    scores = lax.dot_general(both, k, (((1,), (1,)), ((), ())), preferred_element_type=jnp.float32)
    if bias is not None:
        scores = scores + bias
    largest = jnp.max(scores, axis=1, keepdims=True)
    weights = jnp.exp(scores - largest)
    total = jnp.sum(weights, axis=1, keepdims=True)
    out = jnp.dot(weights.astype(jnp.bfloat16), v, preferred_element_type=jnp.float32) / total
    return jnp.where(lane < 64, out[:n], out[n:]).astype(jnp.bfloat16)


def attend_kernel(
    q_ref, k_ref, v_ref, low_ref, high_ref, west_ref, east_ref, bias_ref, out_ref, kbuf, vbuf
):
    width = q_ref.shape[1]
    for buf, own, at in ((kbuf, k_ref, 0), (vbuf, v_ref, 1)):
        buf[0:96] = own[...]
        buf[96:176] = low_ref[at]
        buf[176:256] = high_ref[at]
        buf[256:384] = west_ref[at]
        buf[384:512] = east_ref[at]
    for p in range(width // 128):
        lanes = slice(128 * p, 128 * p + 128)
        q = q_ref[:, lanes] * jnp.bfloat16(0.125)
        bias = bias_ref[2 * p : 2 * p + 2].reshape(2 * CELLS, KEYS)
        out = pair_attention(q, kbuf[:, lanes], vbuf[:, lanes], bias)
        for e in range(2):
            at = turned(2 * p + e) * 64
            out_ref[:, at : at + 64] = out[:, 64 * e : 64 * e + 64]


def turned(chunk):
    return (chunk % 4) * 4 + chunk // 4


def attend(q, k, v, low, high, west, east, bias):
    width = q.shape[1]
    return pl.pallas_call(
        attend_kernel,
        out_shape=jax.ShapeDtypeStruct(q.shape, jnp.bfloat16),
        in_specs=[vspec()] * 8,
        out_specs=vspec(),
        scratch_shapes=[
            pltpu.VMEM((KEYS, width), jnp.bfloat16),
            pltpu.VMEM((KEYS, width), jnp.bfloat16),
        ],
        compiler_params=params(16),
        name="local",
    )(q, k, v, low, high, west, east, bias)


def piece_lanes(at_ref, deep):
    core, x = at_ref[0], at_ref[1]
    half = deep // 2
    far = lax.rem(x + 2, 4) * deep
    starts = (
        x * deep,
        lax.rem(x + 3 + 2 * core, 4) * deep,
        lax.rem(x + 5 - 2 * core, 4) * deep,
        far + core * half,
        far + (1 - core) * half,
    )
    return [pl.ds(pl.multiple_of(start, half), deep if n < 3 else half) for n, start in enumerate(starts)]


def project_kernel(at_ref, x_ref, tok_ref, gain_ref, p0, p1, p2, p3, hid_ref, norm_ref):
    width = x_ref.shape[1]
    total = None
    for lanes, ref in zip(piece_lanes(at_ref, width // 4), unpacked(p0, p1, p2, p3)):
        term = jnp.dot(x_ref[:, lanes], ref[...], preferred_element_type=jnp.float32)
        total = term if total is None else total + term
    hidden = (tok_ref[...].astype(jnp.float32) + total).astype(jnp.bfloat16)
    hid_ref[...] = hidden
    wide = hidden.astype(jnp.float32)
    inverse = lax.rsqrt(jnp.mean(wide * wide, axis=1, keepdims=True) + 1e-06)
    normed = (wide * inverse * gain_ref[...]).astype(jnp.bfloat16)
    for chunk in range(width // 64):
        at = turned(chunk) * 64
        norm_ref[:, at : at + 64] = normed[:, 64 * chunk : 64 * chunk + 64]


def project(at, x, tok, gain, pieces):
    shape = jax.ShapeDtypeStruct(x.shape, jnp.bfloat16)
    return pl.pallas_call(
        project_kernel,
        out_shape=(shape, shape),
        in_specs=[sspec()] + [vspec()] * (3 + len(pieces)),
        out_specs=(vspec(), vspec()),
        compiler_params=params(8),
        name="project",
    )(at, x, tok, gain, *pieces)


def global_kernel(at_ref, own_ref, x1, x2, x3, x4, *rest):
    weights, (out_ref, xbuf) = rest[:15], rest[15:]
    width = own_ref.shape[1]

    @pl.when(pl.program_id(0) == 0)
    def _():
        for at, ref in enumerate((own_ref, x1, x2, x3, x4)):
            xbuf[CELLS * at : CELLS * at + CELLS] = ref[...]

    spans = piece_lanes(at_ref, width // 4)

    def part(rows, refs):
        total = None
        for lanes, ref in zip(spans, refs):
            term = jnp.dot(xbuf[0:rows, lanes], ref[...], preferred_element_type=jnp.float32)
            total = term if total is None else total + term
        return total.astype(jnp.bfloat16)

    q = part(CELLS, weights[0:5]) * jnp.bfloat16(0.125)
    k = part(5 * CELLS, weights[5:10])
    v = part(5 * CELLS, weights[10:15])
    for p in range(q.shape[1] // 128):
        lanes = slice(128 * p, 128 * p + 128)
        out_ref[:, lanes] = pair_attention(q[:, lanes], k[:, lanes], v[:, lanes], None)


def global_layer(at, blocks, pieces):
    cells, width = blocks[0].shape
    steps = width // 256
    whole = [pl.BlockSpec((cells, width), lambda g, c: (0, 0))] * len(blocks)
    weights = [
        pl.BlockSpec((piece.shape[0], 256), lambda g, c, t=t: (0, steps * t + g)) for t in range(3) for piece in pieces
    ]
    return pl.pallas_call(
        global_kernel,
        out_shape=jax.ShapeDtypeStruct((cells, width), jnp.bfloat16),
        grid_spec=pltpu.PrefetchScalarGridSpec(
            num_scalar_prefetch=1,
            grid=(steps,),
            in_specs=whole + weights,
            out_specs=pl.BlockSpec((cells, 256), lambda g, c: (0, g)),
            scratch_shapes=[pltpu.VMEM((5 * cells, width), jnp.bfloat16)],
        ),
        compiler_params=params(20),
        name="global",
    )(at, *blocks, *(pieces * 3))


def place_kernel(at_ref, p0, p1, p2, p3, *rest):
    out_ref = rest[-1]
    rows = p0.shape[0]
    half = rows // 2
    core, zh = at_ref[0], at_ref[2]
    far = lax.rem(zh + 2, 4) * rows
    starts = (
        zh * rows,
        lax.rem(zh + 3 + 2 * core, 4) * rows,
        lax.rem(zh + 5 - 2 * core, 4) * rows,
        far + core * half,
        far + (1 - core) * half,
    )
    for start, ref in zip(starts, unpacked(p0, p1, p2, p3)):
        to = pl.ds(pl.multiple_of(start, half), ref.shape[0])
        out_ref[to] = ref[...]


def place_rows(at, pieces, after):
    rows, columns = pieces[0].shape
    return pl.pallas_call(
        place_kernel,
        out_shape=jax.ShapeDtypeStruct((rows * 4, columns), pieces[0].dtype),
        in_specs=[sspec()] + [vspec()] * len(pieces) + [anyspec()] * len(after),
        out_specs=vspec(),
        compiler_params=params(8),
        name="place",
    )(at, *pieces, *after)


def half_kernel(at_ref, x_ref, *rest):
    out_ref = rest[-1]
    rows = out_ref.shape[0]
    out_ref[...] = x_ref[pl.ds(pl.multiple_of(at_ref[0] * rows, rows), rows)]


def half_of(at, x, after):
    return pl.pallas_call(
        half_kernel,
        out_shape=jax.ShapeDtypeStruct((x.shape[0] // 2, x.shape[1]), x.dtype),
        in_specs=[sspec(), vspec()] + [anyspec()] * len(after),
        out_specs=vspec(),
        compiler_params=params(8),
        name="half",
    )(at, x, *after)


def pack_kernel(a_ref, b_ref, out_ref):
    rows = a_ref.shape[0]
    out_ref[0:rows] = a_ref[...]
    out_ref[rows : rows + b_ref.shape[0]] = b_ref[...]


def pack(a, b):
    return pl.pallas_call(
        pack_kernel,
        out_shape=jax.ShapeDtypeStruct((a.shape[0] + b.shape[0], a.shape[1]), a.dtype),
        in_specs=[vspec(), vspec()],
        out_specs=vspec(),
        compiler_params=params(8),
        name="pack",
    )(a, b)


SWAP = [(0, 1), (1, 0)]
ROLES = [(i, (i + 1) % 4) for i in range(4)] + [(4 + i, 4 + (i + 3) % 4) for i in range(4)]


def gathered(rows, axis, at, after):
    near = lax.ppermute(rows, ("c", axis), ROLES)
    far = lax.ppermute(half_of(at, near, after), ("c", axis), ROLES)
    return [rows, near, far, lax.ppermute(pack(near, far), "c", SWAP)]


def unpacked(own, near, far, others):
    rows = own.shape[0]
    return [own, near, others.at[0:rows], far, others.at[rows : rows + rows // 2]]


def choose_kernel(at_ref, own_ref, behind_ref, after_ref, *outs):
    for by, ref in enumerate(outs, 1):
        ref[...] = jnp.where(at_ref[1] + by < 4, own_ref[...], behind_ref[...])


def choose(at, own, behind, after):
    return pl.pallas_call(
        choose_kernel,
        out_shape=[jax.ShapeDtypeStruct(own.shape, own.dtype)] * 3,
        in_specs=[sspec(), vspec(), vspec(), anyspec()],
        out_specs=[vspec()] * 3,
        compiler_params=params(8),
        name="choose",
    )(at, own, behind, after)


def ring(count, by):
    return [(i, (i + by) % count) for i in range(count)]


def body(tokens, query_local, key_local, value_local, position_bias, output_weight, norm_gain, global_weight):
    width = tokens.shape[2]
    flat = lambda a: a.reshape(CELLS, width)
    q, k, v, tok = flat(query_local), flat(key_local), flat(value_local), flat(tokens)
    core = lax.axis_index("c")
    lat = lax.axis_index(LAT)
    lat_count = lax.axis_size(LAT)
    lon_count = lax.axis_size(LON)
    xs, zs = lax.axis_size("x"), lax.axis_size("zh")
    x, zh = lax.axis_index("x"), lax.axis_index("zh")
    at = jnp.stack([core, x, zh, lat, jnp.int32(lat_count)]).astype(jnp.int32)
    up, down = edges(k, v)
    low = lax.ppermute(up, LAT, [(i, i + 1) for i in range(lat_count - 1)])
    high = lax.ppermute(down, LAT, [(i + 1, i) for i in range(lat_count - 1)])
    bias = bias_table(position_bias, at, up)
    pieces_o = gathered(output_weight, "zh", at, [bias])
    to_east, to_west = sides(low, high, k, v, bias)
    west = lax.ppermute(to_east, LON, ring(lon_count, 1))
    east = lax.ppermute(to_west, LON, ring(lon_count, -1))
    rows_o = place_rows(at, pieces_o, [to_east, to_west])
    global_weight, to_east, pieces_o[2] = lax.optimization_barrier((global_weight, to_east, pieces_o[2]))
    pieces_g = gathered(global_weight, "zh", at, [rows_o])
    pieces_o = gathered(rows_o, "x", at, [west, east])
    local_out = attend(q, k, v, low, high, west, east, bias)
    rows_g = place_rows(at, pieces_g, [pieces_o[2], local_out])
    hidden, normed = project(at, local_out, tok, norm_gain.reshape(1, width), pieces_o)
    behind = lax.ppermute(normed, LON + ("zh",), ring(lon_count * zs, 1))
    near = lax.ppermute(rows_g, ("c", "x"), ROLES)
    half = half_of(at, near, [behind])
    far = lax.ppermute(half, ("c", "x"), ROLES)
    blocks = [normed, behind]
    for by, sent in enumerate(choose(at, normed, behind, half), 1):
        blocks.append(lax.ppermute(sent, "x", ring(xs, by)))
    near_other = lax.ppermute(near, "c", SWAP)
    late, *blocks = lax.optimization_barrier((far, *blocks))
    far_other = lax.ppermute(late, "c", SWAP)
    attended = global_layer(at, blocks, [rows_g, near, near_other, late, far_other])
    return hidden.reshape(tokens.shape), attended.reshape(tokens.shape)


def solution(mesh):
    fine = Mesh(mesh.devices.reshape(2, 8, 2, 4, 4), LON + LAT)
    grid = P(LON, LAT, None)
    return jax.shard_map(
        body,
        mesh=fine,
        in_specs=(grid, grid, grid, grid, P(), P(LAT, None), P(), P(LAT, None)),
        out_specs=(grid, grid),
        check_vma=False,
    )
```
